32 devices in a mesh: groups: 2 (over y), brow: 8 (over z, x), bcol: 2 (over core).
Axes of the slice: x: 2, y: 2, z: 4, core: 2. Of those that a mesh axis runs over, the one named last changes fastest.
Arguments:
- near_pairs: int32 [2048, 2], P(('groups', 'brow', 'bcol')), parts along dimension 0, may hold values from 0 to 255, as said below
- rule_orders: int32 [2048], P(('groups', 'brow', 'bcol')), parts along dimension 0, may hold values from 1 to 3, as said below
- geometry: float32 [6, 131072], P(None, ('groups', 'brow')), parts along dimension 1, may hold values from -1 to 1
- resist: float32 [131072], P(('groups', 'brow')), parts along dimension 0, may hold values from 0.5 to 2
- laplace: float32 [32], replicated, may hold values from 0.002 to 0.02
- right_sides: float32 [32, 131072], P(None, ('groups', 'brow')), parts along dimension 1, may hold values from -40 to 40
Outputs:
- solution: float32 [32, 131072], P(None, ('groups', 'brow')), parts along dimension 1
The draws below stay inside these ranges and needn't reach their ends.
There are 2 independent parts, one for each index of `groups`. The reference program is written for one: setup_inputs(seed, part) draws one part's arguments, and reference() takes and returns one part's arrays. A program takes and returns all parts, laid end to end along the dimension named above; an argument that names none is the same for every part. Nothing has to cross between parts.
Inputs may be any that keep to these rules, and one draw needn't show every extreme that they name: `near_pairs`: the row block i of each pair is owned by brow index i // 32, the brow index of the device that holds the pair; among the 64 pairs of one device at most 16 have column blocks of one owner (column block // 32), and on every device some owner has exactly 16. `rule_orders`: orders may differ from pair to pair and from device to device.
All inputs are finite; a program needn't handle non-finite values.
Results may differ from the reference program's by a relative error of at most 0.0003.
Values sent between devices are 32-bit elements; how exact they have to be, the bound alone decides.
A program may use at most 192 MiB of HBM per device.

```python
import math
import jax
import jax.numpy as jnp
from jax import lax

BS = 256
NRHS = 32
BLK_DEV = 32
PAIRS_DEV = 64
CAP = 16
NB = 256
SEG = 65536
NPAIRS = 1024


def draw_right_sides(key, part):
    key = jax.random.fold_in(key, 11)
    base_key, column_key, segment_key = jax.random.split(key, 3)
    base = jnp.clip(jax.random.normal(base_key, (NRHS, SEG), jnp.float32), -4.0, 4.0)
    column_scale = 10.0 ** jax.random.uniform(column_key, (NRHS, 1), jnp.float32)
    segment_scale = 10.0 ** jax.random.uniform(segment_key, (1, SEG), jnp.float32)
    rising = 1.0 + 2.0 * jnp.arange(SEG, dtype=jnp.float32)[None, :] / SEG
    return base * column_scale * segment_scale * rising / 30.0


def draw_near_pairs(key, part):
    key = jax.random.fold_in(key, 5)
    owners = NB // BLK_DEV
    workers = NPAIRS // PAIRS_DEV
    per_owner = workers // owners
    slot_ids = jnp.arange(owners * CAP, dtype=jnp.int32)

    def one_worker(worker_key, worker):
        full_key, order_key, column_key, row_key, shuffle_key = jax.random.split(worker_key, 5)
        full_owner = jax.random.randint(full_key, (), 0, owners)
        scores = jax.random.permutation(order_key, owners * CAP).astype(jnp.int32)
        priority = jnp.where(slot_ids // CAP == full_owner, slot_ids % CAP - CAP, scores)
        picked = jnp.argsort(priority)[:PAIRS_DEV]
        column = picked // CAP * BLK_DEV + jax.random.randint(column_key, (PAIRS_DEV,), 0, BLK_DEV)
        row = worker // per_owner * BLK_DEV + jax.random.randint(row_key, (PAIRS_DEV,), 0, BLK_DEV)
        listed = jnp.stack([row, column], axis=1).astype(jnp.int32)
        return listed[jax.random.permutation(shuffle_key, PAIRS_DEV)]
    worker_keys = jax.random.split(key, workers)
    return jax.vmap(one_worker)(worker_keys, jnp.arange(workers, dtype=jnp.int32)).reshape(NPAIRS, 2)


def draw_rule_orders(key, part):
    key = jax.random.fold_in(key, 7)
    level_key, order_key, place_key = jax.random.split(key, 3)
    workers = NPAIRS // PAIRS_DEV
    levels = jax.random.randint(level_key, (workers, 1), 0, 3)
    orders = 1 + jax.random.randint(order_key, (workers, PAIRS_DEV), 0, levels + 1)
    place = jax.random.randint(place_key, (), 0, NPAIRS)
    flat = orders.reshape(NPAIRS)
    return jnp.where(jnp.arange(NPAIRS) == place, 3, flat).astype(jnp.int32)


def shard_levels(own_key, dims, cuts, least, largest):
    level = 1.0
    for dim, blocks in cuts:
        heights = jax.random.uniform(jax.random.fold_in(jax.random.fold_in(own_key, 6), dim), (blocks,), jnp.float32, least / len(cuts), largest / len(cuts))
        level = level * jnp.repeat(jnp.exp(heights), dims[dim] // blocks).reshape((-1,) + (1,) * (len(dims) - 1 - dim))
    return level


def setup_inputs(seed: int = 0, part: int = 0) -> dict:
    splits = jax.random.split(jax.random.key(seed), 7)
    part_splits = jax.random.split(jax.random.fold_in(splits[6], part), 7)
    return {
        "near_pairs": draw_near_pairs(jax.random.fold_in(jax.random.fold_in(splits[6], part), 71), part),
        "rule_orders": draw_rule_orders(jax.random.fold_in(jax.random.fold_in(splits[6], part), 71), part),
        "geometry": jnp.clip(jax.random.uniform(part_splits[2], (6, SEG), jnp.float32, -1.0, 1.0) * shard_levels(part_splits[2], (6, SEG), ((1, 8),), -0.4, 0.0), -1.0, 1.0),
        "resist": jnp.clip(jnp.exp(math.log(2.0) - 1.3862944 * jax.random.uniform(part_splits[3], (SEG,), jnp.float32) ** shard_levels(part_splits[3], (SEG,), ((0, 8),), -0.2, 0.2)), 0.5, 2.0),
        "laplace": jnp.clip(jnp.exp(jax.random.uniform(splits[4], (NRHS,), jnp.float32, math.log(0.002), math.log(0.02))), 0.002, 0.02),
        "right_sides": draw_right_sides(jax.random.fold_in(jax.random.fold_in(splits[6], part), 71), part),
    }


RADIUS_SQUARED = 0.0025
GAUSS_TWO = 0.5 / math.sqrt(3.0)
GAUSS_THREE = math.sqrt(0.15)
NODE_TABLE = ((0.0, 0.0, 0.0), (-GAUSS_TWO, GAUSS_TWO, 0.0), (-GAUSS_THREE, 0.0, GAUSS_THREE))
WEIGHT_TABLE = ((1.0, 0.0, 0.0), (0.5, 0.5, 0.0), (5.0 / 18.0, 8.0 / 18.0, 5.0 / 18.0))
EPSILON = 1e-12
PRECISE = lax.Precision.HIGHEST

def rule_terms(rule_orders):
    chosen = (rule_orders[:, None] == jnp.arange(1, 4, dtype=jnp.int32)[None, :]).astype(jnp.float32)
    abscissa = jnp.dot(chosen, jnp.array(NODE_TABLE, jnp.float32), precision=PRECISE)
    weights = jnp.dot(chosen, jnp.array(WEIGHT_TABLE, jnp.float32), precision=PRECISE)
    return (abscissa, weights)

def block_kernel(left_geometry, right_geometry, rule_orders, terms_used):
    abscissa, weights = rule_terms(rule_orders)
    shape_out = (left_geometry.shape[0], left_geometry.shape[2], right_geometry.shape[2])
    summed = jnp.zeros(shape_out, jnp.float32)
    for first_node in range(terms_used):
        for second_node in range(terms_used):
            squared = jnp.full(shape_out, RADIUS_SQUARED, jnp.float32)
            for component in range(3):
                point_left = left_geometry[:, component, :] + abscissa[:, first_node:first_node + 1] * left_geometry[:, component + 3, :]
                point_right = right_geometry[:, component, :] + abscissa[:, second_node:second_node + 1] * right_geometry[:, component + 3, :]
                offset = point_left[:, :, None] - point_right[:, None, :]
                squared = squared + offset * offset
            factor = (weights[:, first_node] * weights[:, second_node])[:, None, None]
            summed = summed + factor * lax.rsqrt(squared)
    tangents = jnp.einsum('gda,gdb->gab', left_geometry[:, 3:6, :], right_geometry[:, 3:6, :], precision=PRECISE)
    return tangents * summed

def near_field(vector, near_pairs, rule_orders, geometry_blocks):
    columns = vector.reshape(NRHS, NB, BS).transpose(1, 0, 2)

    def one_pair(summed, packed):
        couple, order_one = packed
        left_index = couple[0].astype(jnp.int32)
        right_index = couple[1].astype(jnp.int32)
        left_geometry = lax.dynamic_slice_in_dim(geometry_blocks, left_index, 1, 0)
        right_geometry = lax.dynamic_slice_in_dim(geometry_blocks, right_index, 1, 0)
        block = block_kernel(left_geometry, right_geometry, order_one[None], 3)[0]
        forward = jnp.dot(columns[right_index], block.T, precision=PRECISE)
        backward = jnp.dot(columns[left_index], block, precision=PRECISE) * (left_index != right_index).astype(jnp.float32)
        summed = summed.at[left_index].add(forward)
        summed = summed.at[right_index].add(backward)
        return (summed, None)
    summed, unused = lax.scan(one_pair, jnp.zeros((NB, NRHS, BS), jnp.float32), (near_pairs, rule_orders))
    return summed.transpose(1, 0, 2).reshape(NRHS, NB * BS)

def reference(near_pairs, rule_orders, geometry, resist, laplace, right_sides):
    geometry_blocks = geometry.reshape(6, NB, BS).transpose(1, 0, 2)

    def operator(vector):
        return resist[None, :] * vector + laplace[:, None] * near_field(vector, near_pairs, rule_orders, geometry_blocks)

    def product(left, right):
        return lax.optimization_barrier(jnp.sum(left * right, axis=1))
    start_norm = jnp.sqrt(product(right_sides, right_sides) + EPSILON)
    first = right_sides / start_norm[:, None]
    image = operator(first)
    along_first = product(first, image)
    second_raw = image - along_first[:, None] * first
    rest_first = jnp.sqrt(product(second_raw, second_raw) + EPSILON)
    second = second_raw / rest_first[:, None]
    image_two = operator(second)
    along_cross = product(first, image_two)
    along_second = product(second, image_two)
    remainder = image_two - along_cross[:, None] * first - along_second[:, None] * second
    rest_second = jnp.sqrt(product(remainder, remainder) + EPSILON)
    radius_one = jnp.sqrt(along_first * along_first + rest_first * rest_first)
    cosine_one = along_first / radius_one
    sine_one = rest_first / radius_one
    upper_right = cosine_one * along_cross + sine_one * along_second
    lower_right = cosine_one * along_second - sine_one * along_cross
    radius_two = jnp.sqrt(lower_right * lower_right + rest_second * rest_second)
    amount_two = -(lower_right / radius_two) * start_norm * sine_one / radius_two
    amount_one = (start_norm * cosine_one - upper_right * amount_two) / radius_one
    return amount_one[:, None] * first + amount_two[:, None] * second
```

```python
from functools import partial
import math

import jax
import jax.numpy as jnp
from jax import lax
from jax.experimental import pallas as pl
from jax.experimental.pallas import tpu as pltpu
from jax.sharding import PartitionSpec as P

BS = 256


RADIUS_SQUARED = 0.0025
GAUSS_TWO = 0.5 / math.sqrt(3.0)
GAUSS_THREE = math.sqrt(0.15)
NODE_TABLE = ((0.0, 0.0, 0.0), (-GAUSS_TWO, GAUSS_TWO, 0.0), (-GAUSS_THREE, 0.0, GAUSS_THREE))
WEIGHT_TABLE = ((1.0, 0.0, 0.0), (0.5, 0.5, 0.0), (5.0 / 18.0, 8.0 / 18.0, 5.0 / 18.0))
EPSILON = 1e-12
PRECISE = lax.Precision.HIGHEST


def rule_terms(rule_orders):
    chosen = (rule_orders[:, None] == jnp.arange(1, 4, dtype=jnp.int32)[None, :]).astype(
        jnp.float32
    )
    abscissa = jnp.dot(chosen, jnp.array(NODE_TABLE, jnp.float32), precision=PRECISE)
    weights = jnp.dot(chosen, jnp.array(WEIGHT_TABLE, jnp.float32), precision=PRECISE)
    return (abscissa, weights)


def block_kernel(left_geometry, right_geometry, rule_orders, terms_used):
    abscissa, weights = rule_terms(rule_orders)
    shape_out = (left_geometry.shape[0], left_geometry.shape[2], right_geometry.shape[2])
    summed = jnp.zeros(shape_out, jnp.float32)
    for first_node in range(terms_used):
        for second_node in range(terms_used):
            squared = jnp.full(shape_out, RADIUS_SQUARED, jnp.float32)
            for component in range(3):
                point_left = (
                    left_geometry[:, component, :]
                    + abscissa[:, first_node : first_node + 1] * left_geometry[:, component + 3, :]
                )
                point_right = (
                    right_geometry[:, component, :]
                    + abscissa[:, second_node : second_node + 1]
                    * right_geometry[:, component + 3, :]
                )
                offset = point_left[:, :, None] - point_right[:, None, :]
                squared = squared + offset * offset
            factor = (weights[:, first_node] * weights[:, second_node])[:, None, None]
            summed = summed + factor * lax.rsqrt(squared)
    tangents = jnp.einsum(
        "gda,gdb->gab", left_geometry[:, 3:6, :], right_geometry[:, 3:6, :], precision=PRECISE
    )
    return tangents * summed


def build_blocks(left_geometry, right_geometry, rule_orders):
    total_pairs = rule_orders.shape[0]
    group_size = math.gcd(total_pairs, 8)
    batches = total_pairs // group_size
    block_width = left_geometry.shape[2]
    branches = [partial(block_kernel, terms_used=rule_level) for rule_level in (1, 2, 3)]

    def one_group(packed):
        left_part, right_part, order_part = packed
        highest = jnp.clip(jnp.max(order_part), 1, 3) - 1
        return lax.switch(highest, branches, left_part, right_part, order_part)

    packed = (
        left_geometry.reshape(batches, group_size, 6, block_width),
        right_geometry.reshape(batches, group_size, 6, block_width),
        rule_orders.reshape(batches, group_size),
    )
    assembled = lax.map(one_group, packed)
    return assembled.reshape(total_pairs, block_width, block_width)


def plain_body(near_pairs, rule_orders, geometry, resist, laplace, right_sides):
    owners = lax.axis_size("brow")
    here = lax.axis_index("brow")
    block_width = BS
    blocks_here = geometry.shape[1] // block_width
    rhs_count = right_sides.shape[0]
    pair_count = near_pairs.shape[0]
    capacity = max(2, 2 * pair_count // owners)
    slot_count = owners * capacity
    own_geometry = geometry.reshape(6, blocks_here, block_width).transpose(1, 0, 2)
    row_local = near_pairs[:, 0] - here * blocks_here
    column_owner = near_pairs[:, 1] // blocks_here
    column_local = near_pairs[:, 1] % blocks_here
    owner_hits = (column_owner[:, None] == jnp.arange(owners, dtype=jnp.int32)[None, :]).astype(
        jnp.int32
    )
    earlier = jnp.cumsum(owner_hits, axis=0) - owner_hits
    slot_of = column_owner * capacity + jnp.sum(earlier * owner_hits, axis=1)
    distinct = (near_pairs[:, 0] != near_pairs[:, 1]).astype(jnp.int32)
    row_hot = (jnp.arange(blocks_here, dtype=jnp.int32)[:, None] == row_local[None, :]).astype(
        jnp.float32
    )
    row_geometry = own_geometry[row_local]
    request_table = jnp.full((slot_count,), -1, jnp.int32).at[slot_of].set(column_local)
    incoming = lax.all_to_all(
        request_table.reshape(owners, capacity), "brow", split_axis=0, concat_axis=0, tiled=True
    ).reshape(slot_count)
    served = jnp.maximum(incoming, 0)
    live = (incoming >= 0).astype(jnp.float32)
    serve_hot = (jnp.arange(blocks_here, dtype=jnp.int32)[:, None] == incoming[None, :]).astype(
        jnp.float32
    )
    give_geometry = (own_geometry[served] * live[:, None, None]).reshape(
        owners, capacity, 6, block_width
    )
    column_geometry = lax.all_to_all(
        give_geometry, "brow", split_axis=0, concat_axis=0, tiled=True
    ).reshape(slot_count, 6, block_width)[slot_of]
    blocks = build_blocks(row_geometry, column_geometry, rule_orders)
    distinct_float = distinct.astype(jnp.float32)
    resist_blocks = resist.reshape(blocks_here, 1, block_width)
    laplace_rows = laplace.reshape(1, rhs_count, 1)

    def apply_operator(vector):
        give = (vector[served] * live[:, None, None]).reshape(
            owners, capacity, rhs_count, block_width
        )
        row_vectors = vector[row_local]
        fetched = lax.all_to_all(give, "brow", split_axis=0, concat_axis=0, tiled=True)
        column_vectors = fetched.reshape(slot_count, rhs_count, block_width)[slot_of]
        forward = jnp.einsum("pab,pfb->pfa", blocks, column_vectors, precision=PRECISE)
        transposed = (
            jnp.einsum("pab,pfa->pfb", blocks, row_vectors, precision=PRECISE)
            * distinct_float[:, None, None]
        )
        send_back = (
            jnp.zeros((slot_count, rhs_count, block_width), jnp.float32).at[slot_of].set(transposed)
        )
        backward = lax.all_to_all(
            send_back.reshape(owners, capacity, rhs_count, block_width),
            "brow",
            split_axis=0,
            concat_axis=0,
            tiled=True,
        ).reshape(slot_count, rhs_count, block_width)
        local_terms = jnp.einsum("kp,pfa->kfa", row_hot, forward, precision=PRECISE) + jnp.einsum(
            "ks,sfa->kfa", serve_hot, backward, precision=PRECISE
        )
        near_sum = lax.psum(local_terms, "bcol")
        return resist_blocks * vector + laplace_rows * near_sum

    def product(left, right):
        return jnp.sum(left * right, axis=(0, 2))

    start = right_sides.reshape(rhs_count, blocks_here, block_width).transpose(1, 0, 2)
    start_norm = jnp.sqrt(lax.psum(product(start, start), "brow") + EPSILON)
    first = start / start_norm[None, :, None]
    image = apply_operator(first)
    along_first = lax.psum(product(first, image), "brow")
    second_raw = image - along_first[None, :, None] * first
    rest_first = jnp.sqrt(lax.psum(product(second_raw, second_raw), "brow") + EPSILON)
    second = second_raw / rest_first[None, :, None]
    image_two = apply_operator(second)
    along_cross, along_second = lax.psum(
        (product(first, image_two), product(second, image_two)), "brow"
    )
    remainder = (
        image_two - along_cross[None, :, None] * first - along_second[None, :, None] * second
    )
    rest_second = jnp.sqrt(lax.psum(product(remainder, remainder), "brow") + EPSILON)
    radius_one = jnp.sqrt(along_first * along_first + rest_first * rest_first)
    cosine_one = along_first / radius_one
    sine_one = rest_first / radius_one
    upper_right = cosine_one * along_cross + sine_one * along_second
    lower_right = cosine_one * along_second - sine_one * along_cross
    radius_two = jnp.sqrt(lower_right * lower_right + rest_second * rest_second)
    amount_two = -(lower_right / radius_two) * start_norm * sine_one / radius_two
    amount_one = (start_norm * cosine_one - upper_right * amount_two) / radius_one
    combined = amount_one[None, :, None] * first + amount_two[None, :, None] * second
    return combined.transpose(1, 0, 2).reshape(rhs_count, blocks_here * block_width)


MESH = pl.DeviceIdType.MESH
LIMIT = 56 * 1024 * 1024
NODES = ((0.0,), (-GAUSS_TWO, GAUSS_TWO), (-GAUSS_THREE, 0.0, GAUSS_THREE))
WEIGHTS = ((1.0,), (0.5, 0.5), (5.0 / 18.0, 8.0 / 18.0, 5.0 / 18.0))


def ring_place(brow, count):
    return brow // 2 + (brow % 2) * (count - 1 - 2 * (brow // 2))


def ring_owner(place, count):
    upper = place // (count // 2)
    return 2 * place + upper * (2 * (count - 1 - place) + 1 - 2 * place)


def gather_kernel(count, mine_ref, all_ref, own_sem, send_sem, recv_sem, give_sem, take_sem):
    brow, core = lax.axis_index("brow"), lax.axis_index("bcol")
    groups = lax.axis_index("groups")
    place = ring_place(brow, count)
    ahead = ring_owner((place + 1) % count, count)
    behind = ring_owner((place + count - 1) % count, count)
    targets = ((groups, ahead, core), (groups, behind, core))
    other = (groups, brow, 1 - core)
    part = mine_ref.shape[0] // 2
    barrier = pltpu.get_barrier_semaphore()
    for device in targets + (other,):
        pl.semaphore_signal(barrier, inc=1, device_id=device, device_id_type=MESH)
    pl.semaphore_wait(barrier, 3)

    def piece(owner, half):
        return all_ref.at[2 * owner + core, pl.ds(half * part, part)]

    last = count - 2

    def half_of(way, index):
        return (index % 2) if way == 0 else 1 - index % 2

    def owner_of(way, steps):
        shift = count - steps if way == 0 else steps
        return ring_owner((place + shift) % count, count)

    def ring_copy(way, index):
        step, half = index // 2, half_of(way, index)
        owner = owner_of(way, step) if step else brow
        source = piece(owner, half) if step else mine_ref.at[pl.ds(half * part, part)]
        return pltpu.make_async_remote_copy(
            src_ref=source,
            dst_ref=piece(owner, half),
            send_sem=send_sem.at[way, index],
            recv_sem=recv_sem.at[way, index],
            device_id=targets[way],
            device_id_type=MESH,
        )

    def landing(way, index):
        owner, half = owner_of(way, index // 2 + 1), half_of(way, index)
        return pltpu.make_async_remote_copy(
            src_ref=piece(owner, half),
            dst_ref=piece(owner, half),
            send_sem=send_sem.at[way, index],
            recv_sem=recv_sem.at[way, index],
            device_id=targets[way],
            device_id_type=MESH,
        )

    def core_copy(number, source, target):
        return pltpu.make_async_remote_copy(
            src_ref=source,
            dst_ref=target,
            send_sem=give_sem.at[number],
            recv_sem=take_sem.at[number],
            device_id=other,
            device_id_type=MESH,
        )

    own = pltpu.make_async_copy(mine_ref, all_ref.at[2 * brow + core], own_sem)
    own.start()
    sends, gives = [], []
    for index in range(2):
        for way in range(2):
            copy = ring_copy(way, index)
            copy.start()
            sends.append(copy)
    copy = core_copy(0, mine_ref, all_ref.at[2 * brow + core])
    copy.start()
    gives.append(copy)
    for index in range(last + 1):
        for way in range(2):
            landing(way, index).wait_recv()
            if index + 2 <= last:
                copy = ring_copy(way, index + 2)
                copy.start()
                sends.append(copy)
            view = piece(owner_of(way, index // 2 + 1), half_of(way, index))
            copy = core_copy(1 + 2 * index + way, view, view)
            copy.start()
            gives.append(copy)
    own.wait()
    for copy in sends:
        copy.wait_send()
    for number, copy in enumerate(gives):
        copy.wait_send()
        if number == 0:
            target = all_ref.at[2 * brow + 1 - core]
        else:
            way, index = (number - 1) % 2, (number - 1) // 2
            owner, half = owner_of(way, index // 2 + 1), half_of(way, index)
            target = all_ref.at[2 * owner + 1 - core, pl.ds(half * part, part)]
        core_copy(number, target, target).wait_recv()


def gather_all(mine, count, number):
    pieces = 2 * (count - 1)
    return pl.pallas_call(
        partial(gather_kernel, count),
        out_shape=jax.ShapeDtypeStruct((2 * count,) + mine.shape, mine.dtype),
        in_specs=[pl.BlockSpec(memory_space=pl.ANY)],
        out_specs=pl.BlockSpec(memory_space=pl.ANY),
        scratch_shapes=[
            pltpu.SemaphoreType.DMA,
            pltpu.SemaphoreType.DMA((2, count - 1)),
            pltpu.SemaphoreType.DMA((2, count - 1)),
            pltpu.SemaphoreType.DMA((1 + pieces,)),
            pltpu.SemaphoreType.DMA((1 + pieces,)),
        ],
        compiler_params=pltpu.CompilerParams(collective_id=number, has_side_effects=True),
        name="gather_all",
    )(mine)


def sum_kernel(count, part_ref, sum_ref, inbox, send_sem, recv_sem):
    brow, core = lax.axis_index("brow"), lax.axis_index("bcol")
    groups = lax.axis_index("groups")
    here = 2 * brow + core
    total = 2 * count
    barrier = pltpu.get_barrier_semaphore()
    devices = []
    for shift in range(1, total):
        index = (here + shift) % total
        devices.append((groups, index // 2, index % 2))
    for device in devices:
        pl.semaphore_signal(barrier, inc=1, device_id=device, device_id_type=MESH)
    pl.semaphore_wait(barrier, total - 1)
    copies = []
    for shift, device in enumerate(devices):
        copy = pltpu.make_async_remote_copy(
            src_ref=part_ref,
            dst_ref=inbox.at[shift],
            send_sem=send_sem.at[shift],
            recv_sem=recv_sem.at[shift],
            device_id=device,
            device_id_type=MESH,
        )
        copy.start()
        copies.append(copy)
    for copy in copies:
        copy.wait()
    slots = [part_ref[...]] + [inbox[shift] for shift in range(total - 1)]
    result = jnp.zeros_like(slots[0])
    for index in range(total):
        term = jnp.zeros_like(result)
        for shift in range(total):
            source = (here + total - shift) % total
            term = term + jnp.where(source == index, slots[shift], 0.0)
        result = result + term
    sum_ref[...] = result


def sum_all(part, count, number):
    total = 2 * count
    return pl.pallas_call(
        partial(sum_kernel, count),
        out_shape=jax.ShapeDtypeStruct(part.shape, part.dtype),
        in_specs=[pl.BlockSpec(memory_space=pltpu.VMEM)],
        out_specs=pl.BlockSpec(memory_space=pltpu.VMEM),
        scratch_shapes=[
            pltpu.VMEM((total - 1,) + part.shape, part.dtype),
            pltpu.SemaphoreType.DMA((total - 1,)),
            pltpu.SemaphoreType.DMA((total - 1,)),
        ],
        compiler_params=pltpu.CompilerParams(collective_id=number, has_side_effects=True),
        name="sum_all",
    )(part)


def swap_kernel(mine_ref, both_ref, own_sem, send_sem, recv_sem):
    brow, core = lax.axis_index("brow"), lax.axis_index("bcol")
    other = (lax.axis_index("groups"), brow, 1 - core)
    barrier = pltpu.get_barrier_semaphore()
    pl.semaphore_signal(barrier, inc=1, device_id=other, device_id_type=MESH)
    pl.semaphore_wait(barrier, 1)
    copy = pltpu.make_async_remote_copy(
        src_ref=mine_ref,
        dst_ref=both_ref.at[core],
        send_sem=send_sem,
        recv_sem=recv_sem,
        device_id=other,
        device_id_type=MESH,
    )
    copy.start()
    own = pltpu.make_async_copy(mine_ref, both_ref.at[core], own_sem)
    own.start()
    own.wait()
    copy.wait()


def swap_cores(mine, number):
    return pl.pallas_call(
        swap_kernel,
        out_shape=jax.ShapeDtypeStruct((2,) + mine.shape, mine.dtype),
        in_specs=[pl.BlockSpec(memory_space=pl.ANY)],
        out_specs=pl.BlockSpec(memory_space=pl.ANY),
        scratch_shapes=[pltpu.SemaphoreType.DMA] * 3,
        compiler_params=pltpu.CompilerParams(collective_id=number, has_side_effects=True),
        name="swap_cores",
    )(mine)


def multiply(vector, block_ref):
    width = block_ref.shape[1]
    coarse = vector.astype(jnp.bfloat16)
    fine = (vector - coarse.astype(jnp.float32)).astype(jnp.bfloat16)
    rows = vector.shape[0]
    both = jnp.dot(
        jnp.concatenate([coarse, fine], axis=0),
        block_ref[0:width, :],
        preferred_element_type=jnp.float32,
    )
    rest = jnp.dot(coarse, block_ref[width : 2 * width, :], preferred_element_type=jnp.float32)
    return both[:rows] + (both[rows:] + rest)


def build_kernel(first_row, count_ref, source_ref, target_ref, place_ref, order_ref, all_ref, near_ref, blocks_ref, buffer, sems):
    width = near_ref.shape[2]
    rows = near_ref.shape[1]
    near_ref[...] = jnp.zeros_like(near_ref)
    total = count_ref[0]
    tile = 64

    def copy_out(slot, edge):
        return pltpu.make_async_copy(buffer.at[slot], blocks_ref.at[edge], sems.at[slot])

    def one_edge(edge, carry):
        slot = lax.rem(edge, 2)

        @pl.when(edge >= 2)
        def _():
            copy_out(slot, edge - 2).wait()

        source, target, order = source_ref[edge], target_ref[edge], order_ref[edge]
        left = all_ref[source, rows : rows + 8, :]
        right = all_ref[target, rows : rows + 8, :]
        tangent_left = jnp.transpose(left)

        for level in range(3):
            nodes, weights = NODES[level], WEIGHTS[level]

            @pl.when(order == level + 1)
            def _():
                columns = []
                lines = []
                for node in nodes:
                    if node == 0.0:
                        columns.append(tangent_left)
                        lines.append(right[0:3])
                    else:
                        moved = left[0:3] + node * left[3:6]
                        columns.append(
                            jnp.transpose(jnp.concatenate([moved, left[3:8]], axis=0))
                        )
                        lines.append(right[0:3] + node * right[3:6])
                for start in range(0, width, tile):
                    part = slice(start, start + tile)
                    classes = {}
                    for m in range(len(nodes)):
                        for n in range(len(nodes)):
                            squared = None
                            for component in range(3):
                                offset = (
                                    columns[m][part, component : component + 1]
                                    - lines[n][component : component + 1, :]
                                )
                                term = offset * offset
                                squared = term + RADIUS_SQUARED if squared is None else squared + term
                            value = lax.rsqrt(squared)
                            weight = weights[m] * weights[n]
                            classes[weight] = (
                                classes[weight] + value if weight in classes else value
                            )
                    summed = None
                    for weight, value in classes.items():
                        value = value if weight == 1.0 else weight * value
                        summed = value if summed is None else summed + value
                    dots = None
                    for component in range(3, 6):
                        term = (
                            tangent_left[part, component : component + 1]
                            * right[component : component + 1, :]
                        )
                        dots = term if dots is None else dots + term
                    block = dots * summed
                    coarse = block.astype(jnp.bfloat16)
                    fine = (block - coarse.astype(jnp.float32)).astype(jnp.bfloat16)
                    buffer[slot, start : start + tile, :] = coarse
                    buffer[slot, width + start : width + start + tile, :] = fine

        copy_out(slot, edge).start()
        place = place_ref[edge]
        near_ref[place] = near_ref[place] + multiply(all_ref[source, 0:rows, :], buffer.at[slot])
        return carry

    lax.fori_loop(0, total, one_edge, 0)

    @pl.when(total >= 2)
    def _():
        copy_out(lax.rem(total, 2), total - 2).wait()

    @pl.when(total >= 1)
    def _():
        copy_out(lax.rem(total + 1, 2), total - 1).wait()


DEPTH = 4


def apply_kernel(count_ref, source_ref, place_ref, all_ref, blocks_ref, near_ref, buffer, sems):
    near_ref[...] = jnp.zeros_like(near_ref)
    total = count_ref[0]

    def copy_in(edge):
        slot = lax.rem(edge, DEPTH)
        return pltpu.make_async_copy(blocks_ref.at[edge], buffer.at[slot], sems.at[slot])

    for edge in range(DEPTH - 1):

        @pl.when(edge < total)
        def _():
            copy_in(jnp.int32(edge)).start()

    def one_edge(edge, carry):
        @pl.when(edge + DEPTH - 1 < total)
        def _():
            copy_in(edge + DEPTH - 1).start()

        copy_in(edge).wait()
        place = place_ref[edge]
        slot = lax.rem(edge, DEPTH)
        near_ref[place] = near_ref[place] + multiply(all_ref[source_ref[edge]], buffer.at[slot])
        return carry

    lax.fori_loop(0, total, one_edge, 0)


def edge_list(near_pairs, rule_orders, me, half, room):
    row, column = near_pairs[:, 0], near_pairs[:, 1]
    source = jnp.concatenate([column, row])
    target = jnp.concatenate([row, column])
    order = jnp.concatenate([rule_orders, rule_orders])
    mine = target // half == me
    mine = mine & jnp.concatenate([jnp.ones(row.shape, bool), row != column])
    lanes = 128
    grid = mine.astype(jnp.float32).reshape(-1, lanes)
    upper = jnp.triu(jnp.ones((lanes, lanes), jnp.float32), 1)
    lower = jnp.tril(jnp.ones((grid.shape[0], grid.shape[0]), jnp.float32), -1)
    inside = jnp.dot(grid, upper, precision=PRECISE)
    before = jnp.dot(lower, jnp.sum(grid, axis=1, keepdims=True), precision=PRECISE)
    position = (inside + before).reshape(-1).astype(jnp.int32)
    position = jnp.where(mine, position, -1)
    code = (source * half + target % half) * 4 + order
    hit = position[None, :] == jnp.arange(room, dtype=jnp.int32)[:, None]
    picked = jnp.sum(jnp.where(hit, code[None, :], 0), axis=1)
    count = jnp.sum(mine.astype(jnp.int32)).reshape(1)
    order = picked % 4
    place = picked // 4 % half
    return count, picked // (4 * half), me * half + place, place, order


def gather_body(near_pairs, rule_orders, geometry, resist, laplace, right_sides):
    owners = lax.axis_size("brow")
    halves = lax.axis_size("bcol")
    core = lax.axis_index("bcol")
    me = lax.axis_index("brow") * halves + core
    width = BS
    blocks_here = geometry.shape[1] // width
    half = blocks_here // halves
    all_blocks = owners * blocks_here
    rhs_count = right_sides.shape[0]
    pair_count = near_pairs.shape[0]
    capacity = max(2, 2 * pair_count // owners)
    room = halves * pair_count + halves * owners * capacity

    listed = lax.all_gather(
        jnp.concatenate([near_pairs, rule_orders[:, None]], axis=1),
        ("brow", "bcol"),
        axis=0,
        tiled=True,
    )
    count, source, target, place, order = edge_list(listed[:, 0:2], listed[:, 2], me, half, room)

    def own_half(array):
        rows = array.shape[0]
        part = lax.dynamic_slice_in_dim(array, core * half * width, half * width, 1)
        return part.reshape(rows, half, width).transpose(1, 0, 2)

    start = own_half(right_sides)
    shape_own = own_half(geometry)
    mine = jnp.concatenate([start, shape_own, jnp.zeros((half, 2, width), jnp.float32)], axis=1)
    everything = gather_all(mine, owners, 0).reshape(all_blocks, rhs_count + 8, width)
    smem = pl.BlockSpec(memory_space=pltpu.SMEM)
    vmem = pl.BlockSpec(memory_space=pltpu.VMEM)
    hbm = pl.BlockSpec(memory_space=pl.ANY)
    near_shape = jax.ShapeDtypeStruct((half, rhs_count, width), jnp.float32)
    near_start, blocks = pl.pallas_call(
        partial(build_kernel, 0),
        out_shape=(near_shape, jax.ShapeDtypeStruct((room, 2 * width, width), jnp.bfloat16)),
        in_specs=[smem] * 5 + [vmem],
        out_specs=(vmem, hbm),
        scratch_shapes=[
            pltpu.VMEM((2, 2 * width, width), jnp.bfloat16),
            pltpu.SemaphoreType.DMA((2,)),
        ],
        compiler_params=pltpu.CompilerParams(vmem_limit_bytes=LIMIT),
        name="build_blocks",
    )(count, source, target, place, order, everything)

    resist_own = lax.dynamic_slice_in_dim(resist, core * half * width, half * width, 0).reshape(
        half, 1, width
    )
    laplace_rows = laplace.reshape(1, rhs_count, 1)

    def spread(amount):
        return amount[None, :, None]

    def dots(number, *couples):
        parts = [jnp.sum(left * right, axis=(0, 2)) for left, right in couples]
        packed = jnp.zeros((8, 128), jnp.float32)
        packed = packed.at[0 : len(parts), 0:rhs_count].set(jnp.stack(parts))
        total = sum_all(packed, owners, number)
        return [total[row, 0:rhs_count] for row in range(len(parts))]

    image = resist_own * start + laplace_rows * near_start
    everything_two = gather_all(image, owners, 1).reshape(all_blocks, rhs_count, width)
    near_image = pl.pallas_call(
        apply_kernel,
        out_shape=near_shape,
        in_specs=[smem] * 3 + [vmem, hbm],
        out_specs=vmem,
        scratch_shapes=[
            pltpu.VMEM((DEPTH, 2 * width, width), jnp.bfloat16),
            pltpu.SemaphoreType.DMA((DEPTH,)),
        ],
        compiler_params=pltpu.CompilerParams(vmem_limit_bytes=LIMIT),
        name="apply_blocks",
    )(count, source, place, everything_two, blocks)

    start_square, start_image = dots(2, (start, start), (start, image))
    start_norm = jnp.sqrt(start_square + EPSILON)
    first = start / spread(start_norm)
    along_first = start_image / start_norm / start_norm
    second_raw = image / spread(start_norm) - spread(along_first) * first
    (rest_square,) = dots(3, (second_raw, second_raw))
    rest_first = jnp.sqrt(rest_square + EPSILON)
    second = second_raw / spread(rest_first)
    near_second = (
        (near_image - spread(along_first) * near_start) / spread(start_norm) / spread(rest_first)
    )
    image_two = resist_own * second + laplace_rows * near_second
    along_cross, along_second = dots(4, (first, image_two), (second, image_two))
    remainder = image_two - spread(along_cross) * first - spread(along_second) * second
    (last_square,) = dots(5, (remainder, remainder))
    rest_second = jnp.sqrt(last_square + EPSILON)
    radius_one = jnp.sqrt(along_first * along_first + rest_first * rest_first)
    cosine_one = along_first / radius_one
    sine_one = rest_first / radius_one
    upper_right = cosine_one * along_cross + sine_one * along_second
    lower_right = cosine_one * along_second - sine_one * along_cross
    radius_two = jnp.sqrt(lower_right * lower_right + rest_second * rest_second)
    amount_two = -(lower_right / radius_two) * start_norm * sine_one / radius_two
    amount_one = (start_norm * cosine_one - upper_right * amount_two) / radius_one
    combined = spread(amount_one) * first + spread(amount_two) * second
    return (
        swap_cores(combined, 6)
        .reshape(blocks_here, rhs_count, width)
        .transpose(1, 0, 2)
        .reshape(rhs_count, blocks_here * width)
    )


def body(near_pairs, rule_orders, geometry, resist, laplace, right_sides):
    owners = lax.axis_size("brow")
    blocks = geometry.shape[1] // BS * owners
    if owners == 8 and lax.axis_size("bcol") == 2 and blocks <= 256:
        return gather_body(near_pairs, rule_orders, geometry, resist, laplace, right_sides)
    return plain_body(near_pairs, rule_orders, geometry, resist, laplace, right_sides)


def solution(mesh):
    return jax.shard_map(
        body,
        mesh=mesh,
        in_specs=(
            P(("groups", "brow", "bcol"), None),
            P(("groups", "brow", "bcol")),
            P(None, ("groups", "brow")),
            P(("groups", "brow")),
            P(),
            P(None, ("groups", "brow")),
        ),
        out_specs=P(None, ("groups", "brow")),
        check_vma=False,
    )
```

```python
from functools import partial
import math

import jax
import jax.numpy as jnp
from jax import lax
from jax.experimental import pallas as pl
from jax.experimental.pallas import tpu as pltpu
from jax.sharding import PartitionSpec as P

BS = 256


RADIUS_SQUARED = 0.0025
GAUSS_TWO = 0.5 / math.sqrt(3.0)
GAUSS_THREE = math.sqrt(0.15)
NODE_TABLE = ((0.0, 0.0, 0.0), (-GAUSS_TWO, GAUSS_TWO, 0.0), (-GAUSS_THREE, 0.0, GAUSS_THREE))
WEIGHT_TABLE = ((1.0, 0.0, 0.0), (0.5, 0.5, 0.0), (5.0 / 18.0, 8.0 / 18.0, 5.0 / 18.0))
EPSILON = 1e-12
PRECISE = lax.Precision.HIGHEST


def rule_terms(rule_orders):
    chosen = (rule_orders[:, None] == jnp.arange(1, 4, dtype=jnp.int32)[None, :]).astype(
        jnp.float32
    )
    abscissa = jnp.dot(chosen, jnp.array(NODE_TABLE, jnp.float32), precision=PRECISE)
    weights = jnp.dot(chosen, jnp.array(WEIGHT_TABLE, jnp.float32), precision=PRECISE)
    return (abscissa, weights)


def block_kernel(left_geometry, right_geometry, rule_orders, terms_used):
    abscissa, weights = rule_terms(rule_orders)
    shape_out = (left_geometry.shape[0], left_geometry.shape[2], right_geometry.shape[2])
    summed = jnp.zeros(shape_out, jnp.float32)
    for first_node in range(terms_used):
        for second_node in range(terms_used):
            squared = jnp.full(shape_out, RADIUS_SQUARED, jnp.float32)
            for component in range(3):
                point_left = (
                    left_geometry[:, component, :]
                    + abscissa[:, first_node : first_node + 1] * left_geometry[:, component + 3, :]
                )
                point_right = (
                    right_geometry[:, component, :]
                    + abscissa[:, second_node : second_node + 1]
                    * right_geometry[:, component + 3, :]
                )
                offset = point_left[:, :, None] - point_right[:, None, :]
                squared = squared + offset * offset
            factor = (weights[:, first_node] * weights[:, second_node])[:, None, None]
            summed = summed + factor * lax.rsqrt(squared)
    tangents = jnp.einsum(
        "gda,gdb->gab", left_geometry[:, 3:6, :], right_geometry[:, 3:6, :], precision=PRECISE
    )
    return tangents * summed


def build_blocks(left_geometry, right_geometry, rule_orders):
    total_pairs = rule_orders.shape[0]
    group_size = math.gcd(total_pairs, 8)
    batches = total_pairs // group_size
    block_width = left_geometry.shape[2]
    branches = [partial(block_kernel, terms_used=rule_level) for rule_level in (1, 2, 3)]

    def one_group(packed):
        left_part, right_part, order_part = packed
        highest = jnp.clip(jnp.max(order_part), 1, 3) - 1
        return lax.switch(highest, branches, left_part, right_part, order_part)

    packed = (
        left_geometry.reshape(batches, group_size, 6, block_width),
        right_geometry.reshape(batches, group_size, 6, block_width),
        rule_orders.reshape(batches, group_size),
    )
    assembled = lax.map(one_group, packed)
    return assembled.reshape(total_pairs, block_width, block_width)


def plain_body(near_pairs, rule_orders, geometry, resist, laplace, right_sides):
    owners = lax.axis_size("brow")
    here = lax.axis_index("brow")
    block_width = BS
    blocks_here = geometry.shape[1] // block_width
    rhs_count = right_sides.shape[0]
    pair_count = near_pairs.shape[0]
    capacity = max(2, 2 * pair_count // owners)
    slot_count = owners * capacity
    own_geometry = geometry.reshape(6, blocks_here, block_width).transpose(1, 0, 2)
    row_local = near_pairs[:, 0] - here * blocks_here
    column_owner = near_pairs[:, 1] // blocks_here
    column_local = near_pairs[:, 1] % blocks_here
    owner_hits = (column_owner[:, None] == jnp.arange(owners, dtype=jnp.int32)[None, :]).astype(
        jnp.int32
    )
    earlier = jnp.cumsum(owner_hits, axis=0) - owner_hits
    slot_of = column_owner * capacity + jnp.sum(earlier * owner_hits, axis=1)
    distinct = (near_pairs[:, 0] != near_pairs[:, 1]).astype(jnp.int32)
    row_hot = (jnp.arange(blocks_here, dtype=jnp.int32)[:, None] == row_local[None, :]).astype(
        jnp.float32
    )
    row_geometry = own_geometry[row_local]
    request_table = jnp.full((slot_count,), -1, jnp.int32).at[slot_of].set(column_local)
    incoming = lax.all_to_all(
        request_table.reshape(owners, capacity), "brow", split_axis=0, concat_axis=0, tiled=True
    ).reshape(slot_count)
    served = jnp.maximum(incoming, 0)
    live = (incoming >= 0).astype(jnp.float32)
    serve_hot = (jnp.arange(blocks_here, dtype=jnp.int32)[:, None] == incoming[None, :]).astype(
        jnp.float32
    )
    give_geometry = (own_geometry[served] * live[:, None, None]).reshape(
        owners, capacity, 6, block_width
    )
    column_geometry = lax.all_to_all(
        give_geometry, "brow", split_axis=0, concat_axis=0, tiled=True
    ).reshape(slot_count, 6, block_width)[slot_of]
    blocks = build_blocks(row_geometry, column_geometry, rule_orders)
    distinct_float = distinct.astype(jnp.float32)
    resist_blocks = resist.reshape(blocks_here, 1, block_width)
    laplace_rows = laplace.reshape(1, rhs_count, 1)

    def apply_operator(vector):
        give = (vector[served] * live[:, None, None]).reshape(
            owners, capacity, rhs_count, block_width
        )
        row_vectors = vector[row_local]
        fetched = lax.all_to_all(give, "brow", split_axis=0, concat_axis=0, tiled=True)
        column_vectors = fetched.reshape(slot_count, rhs_count, block_width)[slot_of]
        forward = jnp.einsum("pab,pfb->pfa", blocks, column_vectors, precision=PRECISE)
        transposed = (
            jnp.einsum("pab,pfa->pfb", blocks, row_vectors, precision=PRECISE)
            * distinct_float[:, None, None]
        )
        send_back = (
            jnp.zeros((slot_count, rhs_count, block_width), jnp.float32).at[slot_of].set(transposed)
        )
        backward = lax.all_to_all(
            send_back.reshape(owners, capacity, rhs_count, block_width),
            "brow",
            split_axis=0,
            concat_axis=0,
            tiled=True,
        ).reshape(slot_count, rhs_count, block_width)
        local_terms = jnp.einsum("kp,pfa->kfa", row_hot, forward, precision=PRECISE) + jnp.einsum(
            "ks,sfa->kfa", serve_hot, backward, precision=PRECISE
        )
        near_sum = lax.psum(local_terms, "bcol")
        return resist_blocks * vector + laplace_rows * near_sum

    def product(left, right):
        return jnp.sum(left * right, axis=(0, 2))

    start = right_sides.reshape(rhs_count, blocks_here, block_width).transpose(1, 0, 2)
    start_norm = jnp.sqrt(lax.psum(product(start, start), "brow") + EPSILON)
    first = start / start_norm[None, :, None]
    image = apply_operator(first)
    along_first = lax.psum(product(first, image), "brow")
    second_raw = image - along_first[None, :, None] * first
    rest_first = jnp.sqrt(lax.psum(product(second_raw, second_raw), "brow") + EPSILON)
    second = second_raw / rest_first[None, :, None]
    image_two = apply_operator(second)
    along_cross, along_second = lax.psum(
        (product(first, image_two), product(second, image_two)), "brow"
    )
    remainder = (
        image_two - along_cross[None, :, None] * first - along_second[None, :, None] * second
    )
    rest_second = jnp.sqrt(lax.psum(product(remainder, remainder), "brow") + EPSILON)
    radius_one = jnp.sqrt(along_first * along_first + rest_first * rest_first)
    cosine_one = along_first / radius_one
    sine_one = rest_first / radius_one
    upper_right = cosine_one * along_cross + sine_one * along_second
    lower_right = cosine_one * along_second - sine_one * along_cross
    radius_two = jnp.sqrt(lower_right * lower_right + rest_second * rest_second)
    amount_two = -(lower_right / radius_two) * start_norm * sine_one / radius_two
    amount_one = (start_norm * cosine_one - upper_right * amount_two) / radius_one
    combined = amount_one[None, :, None] * first + amount_two[None, :, None] * second
    return combined.transpose(1, 0, 2).reshape(rhs_count, blocks_here * block_width)


MESH = pl.DeviceIdType.MESH
LIMIT = 56 * 1024 * 1024
NODES = ((0.0,), (-GAUSS_TWO, GAUSS_TWO), (-GAUSS_THREE, 0.0, GAUSS_THREE))
WEIGHTS = ((1.0,), (0.5, 0.5), (5.0 / 18.0, 8.0 / 18.0, 5.0 / 18.0))


def ring_place(brow, count):
    return brow // 2 + (brow % 2) * (count - 1 - 2 * (brow // 2))


def ring_owner(place, count):
    upper = place // (count // 2)
    return 2 * place + upper * (2 * (count - 1 - place) + 1 - 2 * place)


def gather_kernel(count, mine_ref, all_ref, own_sem, send_sem, recv_sem, give_sem, take_sem):
    brow, core = lax.axis_index("brow"), lax.axis_index("bcol")
    groups = lax.axis_index("groups")
    place = ring_place(brow, count)
    ahead = ring_owner((place + 1) % count, count)
    behind = ring_owner((place + count - 1) % count, count)
    targets = ((groups, ahead, core), (groups, behind, core))
    other = (groups, brow, 1 - core)
    part = mine_ref.shape[0] // 2
    barrier = pltpu.get_barrier_semaphore()
    for device in targets + (other,):
        pl.semaphore_signal(barrier, inc=1, device_id=device, device_id_type=MESH)
    pl.semaphore_wait(barrier, 3)

    def piece(owner, half):
        return all_ref.at[2 * owner + core, pl.ds(half * part, part)]

    last = count - 2

    def half_of(way, index):
        return (index % 2) if way == 0 else 1 - index % 2

    def owner_of(way, steps):
        shift = count - steps if way == 0 else steps
        return ring_owner((place + shift) % count, count)

    def ring_copy(way, index):
        step, half = index // 2, half_of(way, index)
        owner = owner_of(way, step) if step else brow
        source = piece(owner, half) if step else mine_ref.at[pl.ds(half * part, part)]
        return pltpu.make_async_remote_copy(
            src_ref=source,
            dst_ref=piece(owner, half),
            send_sem=send_sem.at[way, index],
            recv_sem=recv_sem.at[way, index],
            device_id=targets[way],
            device_id_type=MESH,
        )

    def landing(way, index):
        owner, half = owner_of(way, index // 2 + 1), half_of(way, index)
        return pltpu.make_async_remote_copy(
            src_ref=piece(owner, half),
            dst_ref=piece(owner, half),
            send_sem=send_sem.at[way, index],
            recv_sem=recv_sem.at[way, index],
            device_id=targets[way],
            device_id_type=MESH,
        )

    def core_copy(number, source, target):
        return pltpu.make_async_remote_copy(
            src_ref=source,
            dst_ref=target,
            send_sem=give_sem.at[number],
            recv_sem=take_sem.at[number],
            device_id=other,
            device_id_type=MESH,
        )

    own = pltpu.make_async_copy(mine_ref, all_ref.at[2 * brow + core], own_sem)
    own.start()
    sends, gives = [], []
    for index in range(2):
        for way in range(2):
            copy = ring_copy(way, index)
            copy.start()
            sends.append(copy)
    copy = core_copy(0, mine_ref, all_ref.at[2 * brow + core])
    copy.start()
    gives.append(copy)
    for index in range(last + 1):
        for way in range(2):
            landing(way, index).wait_recv()
            if index + 2 <= last:
                copy = ring_copy(way, index + 2)
                copy.start()
                sends.append(copy)
            view = piece(owner_of(way, index // 2 + 1), half_of(way, index))
            copy = core_copy(1 + 2 * index + way, view, view)
            copy.start()
            gives.append(copy)
    own.wait()
    for copy in sends:
        copy.wait_send()
    for number, copy in enumerate(gives):
        copy.wait_send()
        if number == 0:
            target = all_ref.at[2 * brow + 1 - core]
        else:
            way, index = (number - 1) % 2, (number - 1) // 2
            owner, half = owner_of(way, index // 2 + 1), half_of(way, index)
            target = all_ref.at[2 * owner + 1 - core, pl.ds(half * part, part)]
        core_copy(number, target, target).wait_recv()


def gather_all(mine, count, number):
    pieces = 2 * (count - 1)
    return pl.pallas_call(
        partial(gather_kernel, count),
        out_shape=jax.ShapeDtypeStruct((2 * count,) + mine.shape, mine.dtype),
        in_specs=[pl.BlockSpec(memory_space=pl.ANY)],
        out_specs=pl.BlockSpec(memory_space=pl.ANY),
        scratch_shapes=[
            pltpu.SemaphoreType.DMA,
            pltpu.SemaphoreType.DMA((2, count - 1)),
            pltpu.SemaphoreType.DMA((2, count - 1)),
            pltpu.SemaphoreType.DMA((1 + pieces,)),
            pltpu.SemaphoreType.DMA((1 + pieces,)),
        ],
        compiler_params=pltpu.CompilerParams(collective_id=number, has_side_effects=True),
        name="gather_all",
    )(mine)


def finish_kernel(
    count, start_ref, image_ref, near_start_ref, near_image_ref, resist_ref, laplace_ref,
    amounts_ref, outbox, inbox, kept, send_sem, recv_sem,
):
    brow, core = lax.axis_index("brow"), lax.axis_index("bcol")
    groups = lax.axis_index("groups")
    here = 2 * brow + core
    total = 2 * count
    blocks, rhs, width = start_ref.shape
    others = []
    for shift in range(1, total):
        index = (here + shift) % total
        others.append((index, (groups, index // 2, index % 2)))
    barrier = pltpu.get_barrier_semaphore()
    for index, device in others:
        pl.semaphore_signal(barrier, inc=1, device_id=device, device_id_type=MESH)
    outbox[...] = jnp.zeros_like(outbox)
    diagonal = lax.broadcasted_iota(jnp.int32, (rhs, rhs), 0) == lax.broadcasted_iota(
        jnp.int32, (rhs, rhs), 1
    )

    def to_row(column):
        return jnp.sum(jnp.where(diagonal, column, 0.0), axis=0, keepdims=True)

    def to_column(row):
        return jnp.sum(jnp.where(diagonal, row, 0.0), axis=1, keepdims=True)

    def sum_all(number, *parts):
        for place, part in enumerate(parts):
            row = to_row(jnp.sum(part, axis=1, keepdims=True))
            outbox[number, place : place + 1, 0:rhs] = row
        if number == 0:
            pl.semaphore_wait(barrier, total - 1)
        copies = []
        for slot, (index, device) in enumerate(others):
            copy = pltpu.make_async_remote_copy(
                src_ref=outbox.at[number],
                dst_ref=inbox.at[number, here],
                send_sem=send_sem.at[number, slot],
                recv_sem=recv_sem.at[number, here],
                device_id=device,
                device_id_type=MESH,
            )
            copy.start()
            copies.append(copy)
        inbox[number, here] = outbox[number]
        for slot, (index, device) in enumerate(others):
            pltpu.make_async_remote_copy(
                src_ref=outbox.at[number],
                dst_ref=inbox.at[number, index],
                send_sem=send_sem.at[number, slot],
                recv_sem=recv_sem.at[number, index],
                device_id=device,
                device_id_type=MESH,
            ).wait_recv()
        for copy in copies:
            copy.wait_send()
        result = inbox[number, 0]
        for index in range(1, total):
            result = result + inbox[number, index]
        return [to_column(result[place : place + 1, 0:rhs]) for place in range(len(parts))]

    def sweep(terms, outputs):
        sums = [jnp.zeros((rhs, width), jnp.float32)] * outputs
        for block in range(blocks):
            sums = [old + new for old, new in zip(sums, terms(block))]
        return sums

    start_square, start_image = sum_all(
        0,
        *sweep(
            lambda k: (start_ref[k] * start_ref[k], start_ref[k] * image_ref[k]),
            2,
        ),
    )
    start_norm = jnp.sqrt(start_square + EPSILON)
    scale = 1.0 / start_norm
    along_first = start_image * scale * scale

    def second_raw(k):
        return (image_ref[k] - along_first * start_ref[k]) * scale

    (rest_square,) = sum_all(1, *sweep(lambda k: (second_raw(k) * second_raw(k),), 1))
    rest_first = jnp.sqrt(rest_square + EPSILON)
    scale_two = 1.0 / rest_first
    laplace_column = laplace_ref[...]

    def cross(k):
        first = start_ref[k] * scale
        second = second_raw(k) * scale_two
        near_second = (near_image_ref[k] - along_first * near_start_ref[k]) * scale * scale_two
        image_two = resist_ref[k] * second + laplace_column * near_second
        kept[k] = image_two
        return first * image_two, second * image_two

    along_cross, along_second = sum_all(2, *sweep(cross, 2))

    def remain(k):
        first = start_ref[k] * scale
        second = second_raw(k) * scale_two
        rest = kept[k] - along_cross * first - along_second * second
        return (rest * rest,)

    (last_square,) = sum_all(3, *sweep(remain, 1))
    rest_second = jnp.sqrt(last_square + EPSILON)
    radius_one = jnp.sqrt(along_first * along_first + rest_first * rest_first)
    cosine_one = along_first / radius_one
    sine_one = rest_first / radius_one
    upper_right = cosine_one * along_cross + sine_one * along_second
    lower_right = cosine_one * along_second - sine_one * along_cross
    radius_two = jnp.sqrt(lower_right * lower_right + rest_second * rest_second)
    amount_two = -(lower_right / radius_two) * start_norm * sine_one / radius_two
    amount_one = (start_norm * cosine_one - upper_right * amount_two) / radius_one
    amounts_ref[...] = jnp.zeros_like(amounts_ref)
    amounts_ref[0:1, 0:rhs] = to_row(amount_one * scale)
    amounts_ref[1:2, 0:rhs] = to_row(along_first)
    amounts_ref[2:3, 0:rhs] = to_row(amount_two * scale * scale_two)


def finish(start, image, near_start, near_image, resist_own, laplace, count, number):
    total = 2 * count
    return pl.pallas_call(
        partial(finish_kernel, count),
        out_shape=jax.ShapeDtypeStruct((8, 128), jnp.float32),
        in_specs=[pl.BlockSpec(memory_space=pltpu.VMEM)] * 6,
        out_specs=pl.BlockSpec(memory_space=pltpu.VMEM),
        scratch_shapes=[
            pltpu.VMEM((4, 8, 128), jnp.float32),
            pltpu.VMEM((4, total, 8, 128), jnp.float32),
            pltpu.VMEM(start.shape, jnp.float32),
            pltpu.SemaphoreType.DMA((4, total - 1)),
            pltpu.SemaphoreType.DMA((4, total)),
        ],
        compiler_params=pltpu.CompilerParams(collective_id=number, has_side_effects=True),
        name="finish",
    )(start, image, near_start, near_image, resist_own, laplace)


def multiply(vector, block_ref):
    width = block_ref.shape[1]
    coarse = vector.astype(jnp.bfloat16)
    fine = (vector - coarse.astype(jnp.float32)).astype(jnp.bfloat16)
    rows = vector.shape[0]
    both = jnp.dot(
        jnp.concatenate([coarse, fine], axis=0),
        block_ref[0:width, :],
        preferred_element_type=jnp.float32,
    )
    rest = jnp.dot(coarse, block_ref[width : 2 * width, :], preferred_element_type=jnp.float32)
    return both[:rows] + (both[rows:] + rest)


def build_kernel(count_ref, source_ref, target_ref, order_ref, shape_ref, blocks_ref, buffer, sems):
    width = shape_ref.shape[2]
    total = count_ref[0]
    tile = 64

    def copy_out(slot, edge):
        return pltpu.make_async_copy(buffer.at[slot], blocks_ref.at[edge], sems.at[slot])

    def one_edge(edge, carry):
        slot = lax.rem(edge, 2)

        @pl.when(edge >= 2)
        def _():
            copy_out(slot, edge - 2).wait()

        source, target, order = source_ref[edge], target_ref[edge], order_ref[edge]
        left = shape_ref[source]
        right = shape_ref[target]
        tangent_left = jnp.transpose(left)

        for level in range(3):
            nodes, weights = NODES[level], WEIGHTS[level]

            @pl.when(order == level + 1)
            def _():
                columns = []
                lines = []
                for node in nodes:
                    if node == 0.0:
                        columns.append(tangent_left)
                        lines.append(right[0:3])
                    else:
                        moved = left[0:3] + node * left[3:6]
                        columns.append(
                            jnp.transpose(jnp.concatenate([moved, left[3:8]], axis=0))
                        )
                        lines.append(right[0:3] + node * right[3:6])
                for start in range(0, width, tile):
                    part = slice(start, start + tile)
                    classes = {}
                    for m in range(len(nodes)):
                        for n in range(len(nodes)):
                            squared = None
                            for component in range(3):
                                offset = (
                                    columns[m][part, component : component + 1]
                                    - lines[n][component : component + 1, :]
                                )
                                term = offset * offset
                                squared = term + RADIUS_SQUARED if squared is None else squared + term
                            value = lax.rsqrt(squared)
                            weight = weights[m] * weights[n]
                            classes[weight] = (
                                classes[weight] + value if weight in classes else value
                            )
                    summed = None
                    for weight, value in classes.items():
                        value = value if weight == 1.0 else weight * value
                        summed = value if summed is None else summed + value
                    dots = None
                    for component in range(3, 6):
                        term = (
                            tangent_left[part, component : component + 1]
                            * right[component : component + 1, :]
                        )
                        dots = term if dots is None else dots + term
                    block = dots * summed
                    coarse = block.astype(jnp.bfloat16)
                    fine = (block - coarse.astype(jnp.float32)).astype(jnp.bfloat16)
                    buffer[slot, start : start + tile, :] = coarse
                    buffer[slot, width + start : width + start + tile, :] = fine

        copy_out(slot, edge).start()
        return carry

    lax.fori_loop(0, total, one_edge, 0)

    @pl.when(total >= 2)
    def _():
        copy_out(lax.rem(total, 2), total - 2).wait()

    @pl.when(total >= 1)
    def _():
        copy_out(lax.rem(total + 1, 2), total - 1).wait()


DEPTH = 4
BATCH = 4


def apply_kernel(count_ref, source_ref, place_ref, all_ref, blocks_ref, near_ref, buffer, sems):
    near_ref[...] = jnp.zeros_like(near_ref)
    total = count_ref[0]
    batches = (total + BATCH - 1) // BATCH

    def copy_in(batch):
        slot = lax.rem(batch, DEPTH)
        return pltpu.make_async_copy(
            blocks_ref.at[pl.ds(batch * BATCH, BATCH)], buffer.at[slot], sems.at[slot]
        )

    for batch in range(DEPTH - 1):

        @pl.when(batch < batches)
        def _():
            copy_in(jnp.int32(batch)).start()

    def one_batch(batch, carry):
        @pl.when(batch + DEPTH - 1 < batches)
        def _():
            copy_in(batch + DEPTH - 1).start()

        copy_in(batch).wait()
        slot = lax.rem(batch, DEPTH)
        terms = []
        for step in range(BATCH):
            edge = batch * BATCH + step
            term = multiply(all_ref[source_ref[edge]], buffer.at[slot, step])
            terms.append((place_ref[edge], jnp.where(edge < total, term, 0.0)))
        for place, term in terms:
            near_ref[place] = near_ref[place] + term
        return carry

    lax.fori_loop(0, batches, one_batch, 0)


SMEM_SPEC = pl.BlockSpec(memory_space=pltpu.SMEM)
HBM_SPEC = pl.BlockSpec(memory_space=pl.ANY)


def call_build(count, source, target, order, everything):
    blocks, rows, width = everything.shape
    room = source.shape[0]
    return pl.pallas_call(
        build_kernel,
        grid=(1,),
        out_shape=jax.ShapeDtypeStruct((room, 2 * width, width), jnp.bfloat16),
        in_specs=[SMEM_SPEC] * 4
        + [pl.BlockSpec((blocks, 8, width), lambda step: (0, rows // 8 - 1, 0))],
        out_specs=HBM_SPEC,
        scratch_shapes=[
            pltpu.VMEM((2, 2 * width, width), jnp.bfloat16),
            pltpu.SemaphoreType.DMA((2,)),
        ],
        compiler_params=pltpu.CompilerParams(vmem_limit_bytes=LIMIT),
        name="build_blocks",
    )(count, source, target, order, everything)


def call_apply(count, source, place, everything, blocks, half, rhs_count):
    width = everything.shape[2]
    return pl.pallas_call(
        apply_kernel,
        grid=(1,),
        out_shape=jax.ShapeDtypeStruct((half, rhs_count, width), jnp.float32),
        in_specs=[SMEM_SPEC] * 3
        + [
            pl.BlockSpec((everything.shape[0], rhs_count, width), lambda step: (0, 0, 0)),
            HBM_SPEC,
        ],
        out_specs=pl.BlockSpec(memory_space=pltpu.VMEM),
        scratch_shapes=[
            pltpu.VMEM((DEPTH, BATCH, 2 * width, width), jnp.bfloat16),
            pltpu.SemaphoreType.DMA((DEPTH,)),
        ],
        compiler_params=pltpu.CompilerParams(vmem_limit_bytes=LIMIT),
        name="apply_blocks",
    )(count, source, place, everything, blocks)


def edge_list(near_pairs, rule_orders, me, half, room):
    row, column = near_pairs[:, 0], near_pairs[:, 1]
    source = jnp.concatenate([column, row])
    target = jnp.concatenate([row, column])
    order = jnp.concatenate([rule_orders, rule_orders])
    mine = target // half == me
    mine = mine & jnp.concatenate([jnp.ones(row.shape, bool), row != column])
    lanes = 128
    grid = mine.astype(jnp.float32).reshape(-1, lanes)
    upper = jnp.triu(jnp.ones((lanes, lanes), jnp.float32), 1)
    lower = jnp.tril(jnp.ones((grid.shape[0], grid.shape[0]), jnp.float32), -1)
    inside = jnp.dot(grid, upper, precision=PRECISE)
    before = jnp.dot(lower, jnp.sum(grid, axis=1, keepdims=True), precision=PRECISE)
    position = (inside + before).reshape(-1).astype(jnp.int32)
    position = jnp.where(mine, position, -1)
    code = (source * half + target % half) * 4 + order
    hit = position[None, :] == jnp.arange(room, dtype=jnp.int32)[:, None]
    picked = jnp.sum(jnp.where(hit, code[None, :], 0), axis=1)
    count = jnp.sum(mine.astype(jnp.int32)).reshape(1)
    order = picked % 4
    place = picked // 4 % half
    return count, picked // (4 * half), me * half + place, place, order


def gather_body(near_pairs, rule_orders, geometry, resist, laplace, right_sides):
    owners = lax.axis_size("brow")
    halves = lax.axis_size("bcol")
    core = lax.axis_index("bcol")
    me = lax.axis_index("brow") * halves + core
    width = BS
    blocks_here = geometry.shape[1] // width
    half = blocks_here // halves
    all_blocks = owners * blocks_here
    rhs_count = right_sides.shape[0]
    pair_count = near_pairs.shape[0]
    capacity = max(2, 2 * pair_count // owners)
    room = halves * pair_count + halves * owners * capacity

    room = -(-room // BATCH) * BATCH
    here = lax.axis_index("brow")

    def own_half(array):
        rows = array.shape[0]
        part = lax.dynamic_slice_in_dim(array, core * half * width, half * width, 1)
        return part.reshape(rows, half, width).transpose(1, 0, 2)

    start = own_half(right_sides)
    shape_own = own_half(geometry)
    listed = jnp.concatenate([near_pairs[:, 0], near_pairs[:, 1], rule_orders])
    listed = jnp.pad(listed.astype(jnp.float32), (0, width - 3 * pair_count))
    spare = jnp.pad(listed.reshape(1, 1, width), ((0, half - 1), (0, 1), (0, 0)))
    mine = jnp.concatenate([start, shape_own, spare], axis=1)
    gathered = gather_all(mine, owners, 0)
    everything = gathered.reshape(all_blocks, rhs_count + 8, width)
    listed = gathered[:, 0, rhs_count + 6, :].astype(jnp.int32)
    pairs = jnp.stack(
        [
            listed[:, 0:pair_count].reshape(-1),
            listed[:, pair_count : 2 * pair_count].reshape(-1),
        ],
        axis=1,
    )
    orders = listed[:, 2 * pair_count : 3 * pair_count].reshape(-1)
    count, source, target, place, order = edge_list(pairs, orders, me, half, room)
    blocks = call_build(count, source, target, order, everything)
    near_start = call_apply(count, source, place, everything, blocks, half, rhs_count)
    resist_own = lax.dynamic_slice_in_dim(resist, core * half * width, half * width, 0).reshape(
        half, 1, width
    )
    image = resist_own * start + laplace.reshape(1, rhs_count, 1) * near_start
    everything_two = gather_all(image, owners, 1).reshape(all_blocks, rhs_count, width)
    near_image = call_apply(count, source, place, everything_two, blocks, half, rhs_count)
    amounts = finish(
        start, image, near_start, near_image, resist_own, laplace.reshape(rhs_count, 1), owners, 2
    )
    own_image = lax.dynamic_slice_in_dim(everything_two, here * blocks_here, blocks_here, 0)
    own_image = own_image.transpose(1, 0, 2).reshape(rhs_count, blocks_here * width)
    amounts = amounts[0:3, 0:rhs_count, None]
    return amounts[0] * right_sides + amounts[2] * (own_image - amounts[1] * right_sides)


def body(near_pairs, rule_orders, geometry, resist, laplace, right_sides):
    owners = lax.axis_size("brow")
    blocks = geometry.shape[1] // BS * owners
    if owners == 8 and lax.axis_size("bcol") == 2 and blocks <= 256 and near_pairs.shape[0] <= 85:
        return gather_body(near_pairs, rule_orders, geometry, resist, laplace, right_sides)
    return plain_body(near_pairs, rule_orders, geometry, resist, laplace, right_sides)


def solution(mesh):
    return jax.shard_map(
        body,
        mesh=mesh,
        in_specs=(
            P(("groups", "brow", "bcol"), None),
            P(("groups", "brow", "bcol")),
            P(None, ("groups", "brow")),
            P(("groups", "brow")),
            P(),
            P(None, ("groups", "brow")),
        ),
        out_specs=P(None, ("groups", "brow")),
        check_vma=False,
    )
```

```python
from functools import partial
import math

import jax
import jax.numpy as jnp
from jax import lax
from jax.experimental import pallas as pl
from jax.experimental.pallas import tpu as pltpu
from jax.sharding import PartitionSpec as P

BS = 256


RADIUS_SQUARED = 0.0025
GAUSS_TWO = 0.5 / math.sqrt(3.0)
GAUSS_THREE = math.sqrt(0.15)
NODE_TABLE = ((0.0, 0.0, 0.0), (-GAUSS_TWO, GAUSS_TWO, 0.0), (-GAUSS_THREE, 0.0, GAUSS_THREE))
WEIGHT_TABLE = ((1.0, 0.0, 0.0), (0.5, 0.5, 0.0), (5.0 / 18.0, 8.0 / 18.0, 5.0 / 18.0))
EPSILON = 1e-12
PRECISE = lax.Precision.HIGHEST


def rule_terms(rule_orders):
    chosen = (rule_orders[:, None] == jnp.arange(1, 4, dtype=jnp.int32)[None, :]).astype(
        jnp.float32
    )
    abscissa = jnp.dot(chosen, jnp.array(NODE_TABLE, jnp.float32), precision=PRECISE)
    weights = jnp.dot(chosen, jnp.array(WEIGHT_TABLE, jnp.float32), precision=PRECISE)
    return (abscissa, weights)


def block_kernel(left_geometry, right_geometry, rule_orders, terms_used):
    abscissa, weights = rule_terms(rule_orders)
    shape_out = (left_geometry.shape[0], left_geometry.shape[2], right_geometry.shape[2])
    summed = jnp.zeros(shape_out, jnp.float32)
    for first_node in range(terms_used):
        for second_node in range(terms_used):
            squared = jnp.full(shape_out, RADIUS_SQUARED, jnp.float32)
            for component in range(3):
                point_left = (
                    left_geometry[:, component, :]
                    + abscissa[:, first_node : first_node + 1] * left_geometry[:, component + 3, :]
                )
                point_right = (
                    right_geometry[:, component, :]
                    + abscissa[:, second_node : second_node + 1]
                    * right_geometry[:, component + 3, :]
                )
                offset = point_left[:, :, None] - point_right[:, None, :]
                squared = squared + offset * offset
            factor = (weights[:, first_node] * weights[:, second_node])[:, None, None]
            summed = summed + factor * lax.rsqrt(squared)
    tangents = jnp.einsum(
        "gda,gdb->gab", left_geometry[:, 3:6, :], right_geometry[:, 3:6, :], precision=PRECISE
    )
    return tangents * summed


def build_blocks(left_geometry, right_geometry, rule_orders):
    total_pairs = rule_orders.shape[0]
    group_size = math.gcd(total_pairs, 8)
    batches = total_pairs // group_size
    block_width = left_geometry.shape[2]
    branches = [partial(block_kernel, terms_used=rule_level) for rule_level in (1, 2, 3)]

    def one_group(packed):
        left_part, right_part, order_part = packed
        highest = jnp.clip(jnp.max(order_part), 1, 3) - 1
        return lax.switch(highest, branches, left_part, right_part, order_part)

    packed = (
        left_geometry.reshape(batches, group_size, 6, block_width),
        right_geometry.reshape(batches, group_size, 6, block_width),
        rule_orders.reshape(batches, group_size),
    )
    assembled = lax.map(one_group, packed)
    return assembled.reshape(total_pairs, block_width, block_width)


def plain_body(near_pairs, rule_orders, geometry, resist, laplace, right_sides):
    owners = lax.axis_size("brow")
    here = lax.axis_index("brow")
    block_width = BS
    blocks_here = geometry.shape[1] // block_width
    rhs_count = right_sides.shape[0]
    pair_count = near_pairs.shape[0]
    capacity = max(2, 2 * pair_count // owners)
    slot_count = owners * capacity
    own_geometry = geometry.reshape(6, blocks_here, block_width).transpose(1, 0, 2)
    row_local = near_pairs[:, 0] - here * blocks_here
    column_owner = near_pairs[:, 1] // blocks_here
    column_local = near_pairs[:, 1] % blocks_here
    owner_hits = (column_owner[:, None] == jnp.arange(owners, dtype=jnp.int32)[None, :]).astype(
        jnp.int32
    )
    earlier = jnp.cumsum(owner_hits, axis=0) - owner_hits
    slot_of = column_owner * capacity + jnp.sum(earlier * owner_hits, axis=1)
    distinct = (near_pairs[:, 0] != near_pairs[:, 1]).astype(jnp.int32)
    row_hot = (jnp.arange(blocks_here, dtype=jnp.int32)[:, None] == row_local[None, :]).astype(
        jnp.float32
    )
    row_geometry = own_geometry[row_local]
    request_table = jnp.full((slot_count,), -1, jnp.int32).at[slot_of].set(column_local)
    incoming = lax.all_to_all(
        request_table.reshape(owners, capacity), "brow", split_axis=0, concat_axis=0, tiled=True
    ).reshape(slot_count)
    served = jnp.maximum(incoming, 0)
    live = (incoming >= 0).astype(jnp.float32)
    serve_hot = (jnp.arange(blocks_here, dtype=jnp.int32)[:, None] == incoming[None, :]).astype(
        jnp.float32
    )
    give_geometry = (own_geometry[served] * live[:, None, None]).reshape(
        owners, capacity, 6, block_width
    )
    column_geometry = lax.all_to_all(
        give_geometry, "brow", split_axis=0, concat_axis=0, tiled=True
    ).reshape(slot_count, 6, block_width)[slot_of]
    blocks = build_blocks(row_geometry, column_geometry, rule_orders)
    distinct_float = distinct.astype(jnp.float32)
    resist_blocks = resist.reshape(blocks_here, 1, block_width)
    laplace_rows = laplace.reshape(1, rhs_count, 1)

    def apply_operator(vector):
        give = (vector[served] * live[:, None, None]).reshape(
            owners, capacity, rhs_count, block_width
        )
        row_vectors = vector[row_local]
        fetched = lax.all_to_all(give, "brow", split_axis=0, concat_axis=0, tiled=True)
        column_vectors = fetched.reshape(slot_count, rhs_count, block_width)[slot_of]
        forward = jnp.einsum("pab,pfb->pfa", blocks, column_vectors, precision=PRECISE)
        transposed = (
            jnp.einsum("pab,pfa->pfb", blocks, row_vectors, precision=PRECISE)
            * distinct_float[:, None, None]
        )
        send_back = (
            jnp.zeros((slot_count, rhs_count, block_width), jnp.float32).at[slot_of].set(transposed)
        )
        backward = lax.all_to_all(
            send_back.reshape(owners, capacity, rhs_count, block_width),
            "brow",
            split_axis=0,
            concat_axis=0,
            tiled=True,
        ).reshape(slot_count, rhs_count, block_width)
        local_terms = jnp.einsum("kp,pfa->kfa", row_hot, forward, precision=PRECISE) + jnp.einsum(
            "ks,sfa->kfa", serve_hot, backward, precision=PRECISE
        )
        near_sum = lax.psum(local_terms, "bcol")
        return resist_blocks * vector + laplace_rows * near_sum

    def product(left, right):
        return jnp.sum(left * right, axis=(0, 2))

    start = right_sides.reshape(rhs_count, blocks_here, block_width).transpose(1, 0, 2)
    start_norm = jnp.sqrt(lax.psum(product(start, start), "brow") + EPSILON)
    first = start / start_norm[None, :, None]
    image = apply_operator(first)
    along_first = lax.psum(product(first, image), "brow")
    second_raw = image - along_first[None, :, None] * first
    rest_first = jnp.sqrt(lax.psum(product(second_raw, second_raw), "brow") + EPSILON)
    second = second_raw / rest_first[None, :, None]
    image_two = apply_operator(second)
    along_cross, along_second = lax.psum(
        (product(first, image_two), product(second, image_two)), "brow"
    )
    remainder = (
        image_two - along_cross[None, :, None] * first - along_second[None, :, None] * second
    )
    rest_second = jnp.sqrt(lax.psum(product(remainder, remainder), "brow") + EPSILON)
    radius_one = jnp.sqrt(along_first * along_first + rest_first * rest_first)
    cosine_one = along_first / radius_one
    sine_one = rest_first / radius_one
    upper_right = cosine_one * along_cross + sine_one * along_second
    lower_right = cosine_one * along_second - sine_one * along_cross
    radius_two = jnp.sqrt(lower_right * lower_right + rest_second * rest_second)
    amount_two = -(lower_right / radius_two) * start_norm * sine_one / radius_two
    amount_one = (start_norm * cosine_one - upper_right * amount_two) / radius_one
    combined = amount_one[None, :, None] * first + amount_two[None, :, None] * second
    return combined.transpose(1, 0, 2).reshape(rhs_count, blocks_here * block_width)


MESH = pl.DeviceIdType.MESH
LIMIT = 56 * 1024 * 1024
NODES = ((0.0,), (-GAUSS_TWO, GAUSS_TWO), (-GAUSS_THREE, 0.0, GAUSS_THREE))
WEIGHTS = ((1.0,), (0.5, 0.5), (5.0 / 18.0, 8.0 / 18.0, 5.0 / 18.0))


def ring_place(brow, count):
    return brow // 2 + (brow % 2) * (count - 1 - 2 * (brow // 2))


def ring_owner(place, count):
    upper = place // (count // 2)
    return 2 * place + upper * (2 * (count - 1 - place) + 1 - 2 * place)


def gather_kernel(count, mine_ref, all_ref, own_sem, send_sem, recv_sem, give_sem, take_sem):
    brow, core = lax.axis_index("brow"), lax.axis_index("bcol")
    groups = lax.axis_index("groups")
    place = ring_place(brow, count)
    ahead = ring_owner((place + 1) % count, count)
    behind = ring_owner((place + count - 1) % count, count)
    targets = ((groups, ahead, core), (groups, behind, core))
    other = (groups, brow, 1 - core)
    part = mine_ref.shape[0] // 2
    barrier = pltpu.get_barrier_semaphore()
    for device in targets + (other,):
        pl.semaphore_signal(barrier, inc=1, device_id=device, device_id_type=MESH)
    pl.semaphore_wait(barrier, 3)

    def piece(owner, half):
        return all_ref.at[2 * owner + core, pl.ds(half * part, part)]

    last = count - 2

    def half_of(way, index):
        return (index % 2) if way == 0 else 1 - index % 2

    def owner_of(way, steps):
        shift = count - steps if way == 0 else steps
        return ring_owner((place + shift) % count, count)

    def ring_copy(way, index):
        step, half = index // 2, half_of(way, index)
        owner = owner_of(way, step) if step else brow
        source = piece(owner, half) if step else mine_ref.at[pl.ds(half * part, part)]
        return pltpu.make_async_remote_copy(
            src_ref=source,
            dst_ref=piece(owner, half),
            send_sem=send_sem.at[way, index],
            recv_sem=recv_sem.at[way, index],
            device_id=targets[way],
            device_id_type=MESH,
        )

    def landing(way, index):
        owner, half = owner_of(way, index // 2 + 1), half_of(way, index)
        return pltpu.make_async_remote_copy(
            src_ref=piece(owner, half),
            dst_ref=piece(owner, half),
            send_sem=send_sem.at[way, index],
            recv_sem=recv_sem.at[way, index],
            device_id=targets[way],
            device_id_type=MESH,
        )

    def core_copy(number, source, target):
        return pltpu.make_async_remote_copy(
            src_ref=source,
            dst_ref=target,
            send_sem=give_sem.at[number],
            recv_sem=take_sem.at[number],
            device_id=other,
            device_id_type=MESH,
        )

    own = pltpu.make_async_copy(mine_ref, all_ref.at[2 * brow + core], own_sem)
    own.start()
    sends, gives = [], []
    for index in range(2):
        for way in range(2):
            copy = ring_copy(way, index)
            copy.start()
            sends.append(copy)
    copy = core_copy(0, mine_ref, all_ref.at[2 * brow + core])
    copy.start()
    gives.append(copy)
    for index in range(last + 1):
        for way in range(2):
            landing(way, index).wait_recv()
            if index + 2 <= last:
                copy = ring_copy(way, index + 2)
                copy.start()
                sends.append(copy)
            view = piece(owner_of(way, index // 2 + 1), half_of(way, index))
            copy = core_copy(1 + 2 * index + way, view, view)
            copy.start()
            gives.append(copy)
    own.wait()
    for copy in sends:
        copy.wait_send()
    for number, copy in enumerate(gives):
        copy.wait_send()
        if number == 0:
            target = all_ref.at[2 * brow + 1 - core]
        else:
            way, index = (number - 1) % 2, (number - 1) // 2
            owner, half = owner_of(way, index // 2 + 1), half_of(way, index)
            target = all_ref.at[2 * owner + 1 - core, pl.ds(half * part, part)]
        core_copy(number, target, target).wait_recv()


def gather_all(mine, count, number):
    pieces = 2 * (count - 1)
    return pl.pallas_call(
        partial(gather_kernel, count),
        out_shape=jax.ShapeDtypeStruct((2 * count,) + mine.shape, mine.dtype),
        in_specs=[pl.BlockSpec(memory_space=pl.ANY)],
        out_specs=pl.BlockSpec(memory_space=pl.ANY),
        scratch_shapes=[
            pltpu.SemaphoreType.DMA,
            pltpu.SemaphoreType.DMA((2, count - 1)),
            pltpu.SemaphoreType.DMA((2, count - 1)),
            pltpu.SemaphoreType.DMA((1 + pieces,)),
            pltpu.SemaphoreType.DMA((1 + pieces,)),
        ],
        compiler_params=pltpu.CompilerParams(collective_id=number, has_side_effects=True),
        name="gather_all",
    )(mine)


def finish_kernel(
    count, start_ref, image_ref, near_start_ref, near_image_ref, resist_ref, laplace_ref,
    amounts_ref, outbox, inbox, kept, send_sem, recv_sem,
):
    brow, core = lax.axis_index("brow"), lax.axis_index("bcol")
    groups = lax.axis_index("groups")
    here = 2 * brow + core
    total = 2 * count
    blocks, rhs, width = start_ref.shape
    others = []
    for shift in range(1, total):
        index = (here + shift) % total
        others.append((index, (groups, index // 2, index % 2)))
    barrier = pltpu.get_barrier_semaphore()
    for index, device in others:
        pl.semaphore_signal(barrier, inc=1, device_id=device, device_id_type=MESH)
    outbox[...] = jnp.zeros_like(outbox)
    diagonal = lax.broadcasted_iota(jnp.int32, (rhs, rhs), 0) == lax.broadcasted_iota(
        jnp.int32, (rhs, rhs), 1
    )

    def to_row(column):
        return jnp.sum(jnp.where(diagonal, column, 0.0), axis=0, keepdims=True)

    def to_column(row):
        return jnp.sum(jnp.where(diagonal, row, 0.0), axis=1, keepdims=True)

    def sum_all(number, *parts):
        for place, part in enumerate(parts):
            row = to_row(jnp.sum(part, axis=1, keepdims=True))
            outbox[number, place : place + 1, 0:rhs] = row
        if number == 0:
            pl.semaphore_wait(barrier, total - 1)
        copies = []
        for slot, (index, device) in enumerate(others):
            copy = pltpu.make_async_remote_copy(
                src_ref=outbox.at[number],
                dst_ref=inbox.at[number, here],
                send_sem=send_sem.at[number, slot],
                recv_sem=recv_sem.at[number, here],
                device_id=device,
                device_id_type=MESH,
            )
            copy.start()
            copies.append(copy)
        inbox[number, here] = outbox[number]
        for slot, (index, device) in enumerate(others):
            pltpu.make_async_remote_copy(
                src_ref=outbox.at[number],
                dst_ref=inbox.at[number, index],
                send_sem=send_sem.at[number, slot],
                recv_sem=recv_sem.at[number, index],
                device_id=device,
                device_id_type=MESH,
            ).wait_recv()
        for copy in copies:
            copy.wait_send()
        result = inbox[number, 0]
        for index in range(1, total):
            result = result + inbox[number, index]
        return [to_column(result[place : place + 1, 0:rhs]) for place in range(len(parts))]

    def sweep(terms, outputs):
        sums = [jnp.zeros((rhs, width), jnp.float32)] * outputs
        for block in range(blocks):
            sums = [old + new for old, new in zip(sums, terms(block))]
        return sums

    start_square, start_image = sum_all(
        0,
        *sweep(
            lambda k: (start_ref[k] * start_ref[k], start_ref[k] * image_ref[k]),
            2,
        ),
    )
    start_norm = jnp.sqrt(start_square + EPSILON)
    scale = 1.0 / start_norm
    along_first = start_image * scale * scale

    def second_raw(k):
        return (image_ref[k] - along_first * start_ref[k]) * scale

    (rest_square,) = sum_all(1, *sweep(lambda k: (second_raw(k) * second_raw(k),), 1))
    rest_first = jnp.sqrt(rest_square + EPSILON)
    scale_two = 1.0 / rest_first
    laplace_column = laplace_ref[...]

    def cross(k):
        first = start_ref[k] * scale
        second = second_raw(k) * scale_two
        near_second = (near_image_ref[k] - along_first * near_start_ref[k]) * scale * scale_two
        image_two = resist_ref[k] * second + laplace_column * near_second
        kept[k] = image_two
        return first * image_two, second * image_two

    along_cross, along_second = sum_all(2, *sweep(cross, 2))

    def remain(k):
        first = start_ref[k] * scale
        second = second_raw(k) * scale_two
        rest = kept[k] - along_cross * first - along_second * second
        return (rest * rest,)

    (last_square,) = sum_all(3, *sweep(remain, 1))
    rest_second = jnp.sqrt(last_square + EPSILON)
    radius_one = jnp.sqrt(along_first * along_first + rest_first * rest_first)
    cosine_one = along_first / radius_one
    sine_one = rest_first / radius_one
    upper_right = cosine_one * along_cross + sine_one * along_second
    lower_right = cosine_one * along_second - sine_one * along_cross
    radius_two = jnp.sqrt(lower_right * lower_right + rest_second * rest_second)
    amount_two = -(lower_right / radius_two) * start_norm * sine_one / radius_two
    amount_one = (start_norm * cosine_one - upper_right * amount_two) / radius_one
    amounts_ref[...] = jnp.zeros_like(amounts_ref)
    amounts_ref[0:1, 0:rhs] = to_row(amount_one * scale)
    amounts_ref[1:2, 0:rhs] = to_row(along_first)
    amounts_ref[2:3, 0:rhs] = to_row(amount_two * scale * scale_two)


def finish(start, image, near_start, near_image, resist_own, laplace, count, number):
    total = 2 * count
    return pl.pallas_call(
        partial(finish_kernel, count),
        out_shape=jax.ShapeDtypeStruct((8, 128), jnp.float32),
        in_specs=[pl.BlockSpec(memory_space=pltpu.VMEM)] * 6,
        out_specs=pl.BlockSpec(memory_space=pltpu.VMEM),
        scratch_shapes=[
            pltpu.VMEM((4, 8, 128), jnp.float32),
            pltpu.VMEM((4, total, 8, 128), jnp.float32),
            pltpu.VMEM(start.shape, jnp.float32),
            pltpu.SemaphoreType.DMA((4, total - 1)),
            pltpu.SemaphoreType.DMA((4, total)),
        ],
        compiler_params=pltpu.CompilerParams(collective_id=number, has_side_effects=True),
        name="finish",
    )(start, image, near_start, near_image, resist_own, laplace)


def multiply(vector, block_ref):
    width = block_ref.shape[1]
    coarse = vector.astype(jnp.bfloat16)
    fine = (vector - coarse.astype(jnp.float32)).astype(jnp.bfloat16)
    rows = vector.shape[0]
    both = jnp.dot(
        jnp.concatenate([coarse, fine], axis=0),
        block_ref[0:width, :],
        preferred_element_type=jnp.float32,
    )
    rest = jnp.dot(coarse, block_ref[width : 2 * width, :], preferred_element_type=jnp.float32)
    return both[:rows] + (both[rows:] + rest)


SLOTS = 4


def build_kernel(count_ref, source_ref, target_ref, order_ref, shape_ref, blocks_ref, buffer, sems):
    width = shape_ref.shape[2]
    total = count_ref[0]
    tile = 64

    def copy_out(slot, edge):
        return pltpu.make_async_copy(buffer.at[slot], blocks_ref.at[edge], sems.at[slot])

    def one_edge(edge, carry):
        slot = lax.rem(edge, SLOTS)

        @pl.when(edge >= SLOTS)
        def _():
            copy_out(slot, edge - SLOTS).wait()

        source, target, order = source_ref[edge], target_ref[edge], order_ref[edge]
        left = shape_ref[source]
        right = shape_ref[target]
        for level in range(3):
            nodes, weights = NODES[level], WEIGHTS[level]

            @pl.when(order == level + 1)
            def _():
                stacked = [left[3:6]]
                lines = []
                for node in nodes:
                    if node == 0.0:
                        stacked.append(left[0:3])
                        lines.append(right[0:3])
                    else:
                        stacked.append(left[0:3] + node * left[3:6])
                        lines.append(right[0:3] + node * right[3:6])
                filled = 3 * len(stacked)
                padded = -(-filled // 8) * 8
                stacked.append(jnp.zeros((padded - filled, width), jnp.float32))
                columns = jnp.transpose(jnp.concatenate(stacked, axis=0))
                for start in range(0, width, tile):
                    part = slice(start, start + tile)
                    classes = {}
                    for m in range(len(nodes)):
                        for n in range(len(nodes)):
                            squared = None
                            for component in range(3):
                                offset = (
                                    columns[part, 3 * m + 3 + component : 3 * m + 4 + component]
                                    - lines[n][component : component + 1, :]
                                )
                                term = offset * offset
                                squared = term + RADIUS_SQUARED if squared is None else squared + term
                            value = lax.rsqrt(squared)
                            weight = weights[m] * weights[n]
                            classes[weight] = (
                                classes[weight] + value if weight in classes else value
                            )
                    summed = None
                    for weight, value in classes.items():
                        value = value if weight == 1.0 else weight * value
                        summed = value if summed is None else summed + value
                    dots = None
                    for component in range(3):
                        term = (
                            columns[part, component : component + 1]
                            * right[component + 3 : component + 4, :]
                        )
                        dots = term if dots is None else dots + term
                    block = dots * summed
                    coarse = block.astype(jnp.bfloat16)
                    fine = (block - coarse.astype(jnp.float32)).astype(jnp.bfloat16)
                    buffer[slot, start : start + tile, :] = coarse
                    buffer[slot, width + start : width + start + tile, :] = fine

        copy_out(slot, edge).start()
        return carry

    lax.fori_loop(0, total, one_edge, 0)

    for back in range(1, SLOTS + 1):

        @pl.when(total >= back)
        def _():
            copy_out(lax.rem(total - back, SLOTS), total - back).wait()


DEPTH = 4
BATCH = 4


def apply_kernel(count_ref, source_ref, place_ref, all_ref, blocks_ref, near_ref, buffer, sems):
    near_ref[...] = jnp.zeros_like(near_ref)
    total = count_ref[0]
    batches = (total + BATCH - 1) // BATCH

    def copy_in(batch):
        slot = lax.rem(batch, DEPTH)
        return pltpu.make_async_copy(
            blocks_ref.at[pl.ds(batch * BATCH, BATCH)], buffer.at[slot], sems.at[slot]
        )

    for batch in range(DEPTH - 1):

        @pl.when(batch < batches)
        def _():
            copy_in(jnp.int32(batch)).start()

    def one_batch(batch, carry):
        @pl.when(batch + DEPTH - 1 < batches)
        def _():
            copy_in(batch + DEPTH - 1).start()

        copy_in(batch).wait()
        slot = lax.rem(batch, DEPTH)
        terms = []
        for step in range(BATCH):
            edge = batch * BATCH + step
            term = multiply(all_ref[source_ref[edge]], buffer.at[slot, step])
            terms.append((place_ref[edge], jnp.where(edge < total, term, 0.0)))
        for place, term in terms:
            near_ref[place] = near_ref[place] + term
        return carry

    lax.fori_loop(0, batches, one_batch, 0)


SMEM_SPEC = pl.BlockSpec(memory_space=pltpu.SMEM)
HBM_SPEC = pl.BlockSpec(memory_space=pl.ANY)


def call_build(count, source, target, order, everything):
    blocks, rows, width = everything.shape
    room = source.shape[0]
    return pl.pallas_call(
        build_kernel,
        grid=(1,),
        out_shape=jax.ShapeDtypeStruct((room, 2 * width, width), jnp.bfloat16),
        in_specs=[SMEM_SPEC] * 4
        + [pl.BlockSpec((blocks, 8, width), lambda step: (0, rows // 8 - 1, 0))],
        out_specs=HBM_SPEC,
        scratch_shapes=[
            pltpu.VMEM((SLOTS, 2 * width, width), jnp.bfloat16),
            pltpu.SemaphoreType.DMA((SLOTS,)),
        ],
        compiler_params=pltpu.CompilerParams(vmem_limit_bytes=LIMIT),
        name="build_blocks",
    )(count, source, target, order, everything)


def call_apply(count, source, place, everything, blocks, half, rhs_count):
    width = everything.shape[2]
    return pl.pallas_call(
        apply_kernel,
        grid=(1,),
        out_shape=jax.ShapeDtypeStruct((half, rhs_count, width), jnp.float32),
        in_specs=[SMEM_SPEC] * 3
        + [
            pl.BlockSpec((everything.shape[0], rhs_count, width), lambda step: (0, 0, 0)),
            HBM_SPEC,
        ],
        out_specs=pl.BlockSpec(memory_space=pltpu.VMEM),
        scratch_shapes=[
            pltpu.VMEM((DEPTH, BATCH, 2 * width, width), jnp.bfloat16),
            pltpu.SemaphoreType.DMA((DEPTH,)),
        ],
        compiler_params=pltpu.CompilerParams(vmem_limit_bytes=LIMIT),
        name="apply_blocks",
    )(count, source, place, everything, blocks)


def edge_list(near_pairs, rule_orders, me, half, room):
    row, column = near_pairs[:, 0], near_pairs[:, 1]
    source = jnp.concatenate([column, row])
    target = jnp.concatenate([row, column])
    order = jnp.concatenate([rule_orders, rule_orders])
    mine = target // half == me
    mine = mine & jnp.concatenate([jnp.ones(row.shape, bool), row != column])
    lanes = 128
    grid = mine.astype(jnp.float32).reshape(-1, lanes)
    upper = jnp.triu(jnp.ones((lanes, lanes), jnp.float32), 1)
    lower = jnp.tril(jnp.ones((grid.shape[0], grid.shape[0]), jnp.float32), -1)
    inside = jnp.dot(grid, upper, precision=PRECISE)
    before = jnp.dot(lower, jnp.sum(grid, axis=1, keepdims=True), precision=PRECISE)
    position = (inside + before).reshape(-1).astype(jnp.int32)
    position = jnp.where(mine, position, -1)
    code = (source * half + target % half) * 4 + order
    hit = position[None, :] == jnp.arange(room, dtype=jnp.int32)[:, None]
    picked = jnp.sum(jnp.where(hit, code[None, :], 0), axis=1)
    count = jnp.sum(mine.astype(jnp.int32)).reshape(1)
    order = picked % 4
    place = picked // 4 % half
    return count, picked // (4 * half), me * half + place, place, order


def gather_body(near_pairs, rule_orders, geometry, resist, laplace, right_sides):
    owners = lax.axis_size("brow")
    halves = lax.axis_size("bcol")
    core = lax.axis_index("bcol")
    me = lax.axis_index("brow") * halves + core
    width = BS
    blocks_here = geometry.shape[1] // width
    half = blocks_here // halves
    all_blocks = owners * blocks_here
    rhs_count = right_sides.shape[0]
    pair_count = near_pairs.shape[0]
    capacity = max(2, 2 * pair_count // owners)
    room = halves * pair_count + halves * owners * capacity

    room = -(-room // BATCH) * BATCH
    here = lax.axis_index("brow")

    def own_half(array):
        rows = array.shape[0]
        part = lax.dynamic_slice_in_dim(array, core * half * width, half * width, 1)
        return part.reshape(rows, half, width).transpose(1, 0, 2)

    start = own_half(right_sides)
    shape_own = own_half(geometry)
    listed = jnp.concatenate([near_pairs[:, 0], near_pairs[:, 1], rule_orders])
    listed = jnp.pad(listed.astype(jnp.float32), (0, width - 3 * pair_count))
    spare = jnp.pad(listed.reshape(1, 1, width), ((0, half - 1), (0, 1), (0, 0)))
    mine = jnp.concatenate([start, shape_own, spare], axis=1)
    gathered = gather_all(mine, owners, 0)
    everything = gathered.reshape(all_blocks, rhs_count + 8, width)
    listed = gathered[:, 0, rhs_count + 6, :].astype(jnp.int32)
    pairs = jnp.stack(
        [
            listed[:, 0:pair_count].reshape(-1),
            listed[:, pair_count : 2 * pair_count].reshape(-1),
        ],
        axis=1,
    )
    orders = listed[:, 2 * pair_count : 3 * pair_count].reshape(-1)
    count, source, target, place, order = edge_list(pairs, orders, me, half, room)
    blocks = call_build(count, source, target, order, everything)
    near_start = call_apply(count, source, place, everything, blocks, half, rhs_count)
    resist_own = lax.dynamic_slice_in_dim(resist, core * half * width, half * width, 0).reshape(
        half, 1, width
    )
    image = resist_own * start + laplace.reshape(1, rhs_count, 1) * near_start
    everything_two = gather_all(image, owners, 1).reshape(all_blocks, rhs_count, width)
    near_image = call_apply(count, source, place, everything_two, blocks, half, rhs_count)
    amounts = finish(
        start, image, near_start, near_image, resist_own, laplace.reshape(rhs_count, 1), owners, 2
    )
    own_image = lax.dynamic_slice_in_dim(everything_two, here * blocks_here, blocks_here, 0)
    own_image = own_image.transpose(1, 0, 2).reshape(rhs_count, blocks_here * width)
    amounts = amounts[0:3, 0:rhs_count, None]
    return amounts[0] * right_sides + amounts[2] * (own_image - amounts[1] * right_sides)


def body(near_pairs, rule_orders, geometry, resist, laplace, right_sides):
    owners = lax.axis_size("brow")
    blocks = geometry.shape[1] // BS * owners
    if owners == 8 and lax.axis_size("bcol") == 2 and blocks <= 256 and near_pairs.shape[0] <= 85:
        return gather_body(near_pairs, rule_orders, geometry, resist, laplace, right_sides)
    return plain_body(near_pairs, rule_orders, geometry, resist, laplace, right_sides)


def solution(mesh):
    return jax.shard_map(
        body,
        mesh=mesh,
        in_specs=(
            P(("groups", "brow", "bcol"), None),
            P(("groups", "brow", "bcol")),
            P(None, ("groups", "brow")),
            P(("groups", "brow")),
            P(),
            P(None, ("groups", "brow")),
        ),
        out_specs=P(None, ("groups", "brow")),
        check_vma=False,
    )
```
